128 devices in a mesh: section: 4 (over x), expert: 32 (over y, z, core).
Axes of the slice: x: 4, y: 4, z: 4, core: 2. Of those that a mesh axis runs over, the one named last changes fastest.
Arguments:
- section_input: bfloat16 [4, 4096, 2048], P('section', 'expert'), may hold values from -6 to 6
- fresh_batch: bfloat16 [4096, 2048], P('expert'), may hold values from -6 to 6
- attn_gain: float32 [4, 2048], P('section'), may hold values from 0.1 to 1.9
- query_gain: float32 [4, 64], P('section'), may hold values from 0.5 to 1.5
- key_gain: float32 [4, 64], P('section'), may hold values from 0.5 to 1.5
- kv_weight: bfloat16 [4, 2048, 512], P('section'), may hold values from -0.125 to 0.125
- out_weight: bfloat16 [4, 2048, 2048], P('section', 'expert'), may hold values from -0.125 to 0.125
- moe_gain: float32 [4, 2048], P('section'), may hold values from 0.1 to 1.9
- expert_gate_up: bfloat16 [4, 64, 2048, 1536], P('section', 'expert'), may hold values from -0.125 to 0.125
- expert_down: bfloat16 [4, 64, 768, 2048], P('section', 'expert'), may hold values from -0.21875 to 0.21875
- route_ids: int32 [4, 2, 4096, 8], P('section', None, 'expert'), may hold values from 0 to 63, all different within a row; in each aligned block of 128 rows (0 to 127, 128 to 255, ..., all dimensions but the last counted through in order) at most 18 rows name the same one
- route_weights: int32 [4, 2, 4096, 8], P('section', None, 'expert'), may hold values from 1 to 255
Outputs:
- layer_first: bfloat16 [4, 4096, 2048], P('section', 'expert')
- layer_second: bfloat16 [4, 4096, 2048], P('section', 'expert')
The draws below stay inside these ranges and needn't reach their ends.
Inputs may be any that keep to these rules, and one draw needn't show every extreme that they name: `route_ids`: each row names 8 different experts. In the rows of one device (aligned blocks of 128 rows of one section and tick) no expert is named more than 18 times; one expert is named exactly 18 times in some or all blocks.
All inputs are finite; a program needn't handle non-finite values.
Results may differ from the reference program's by a relative error of at most 0.015.
Values may be sent and summed in bfloat16 or wider, within the bound.
A program may use at most 256 MiB of HBM per device.

```python
import math
import jax
import jax.numpy as jnp
import numpy as np
from jax import lax

D = 2048
HEAD = 64
QH = 32
KVH = 4
FF = 768
TOPK = 8
TOK_DEV = 128
SECTIONS = 4
TOKENS = 4096
SEQ_LEN = 4096
EXPERTS = 64
CAP = 18
N_EXPERT = 32


def with_ends(entries, rng, least, largest):
    longest = entries.shape.index(max(entries.shape))
    spots = []
    for shift in (0, 1):
        where = [jax.random.randint(jax.random.fold_in(rng, axis), (), 0, length) for axis, length in enumerate(entries.shape)]
        where[longest] = (where[longest] + shift) % entries.shape[longest]
        spots.append(tuple(where))
    return entries.at[spots[0]].set(least).at[spots[1]].set(largest)


def steps_of(stream_key, dims, split, low, high):
    def one(axis_at, parts):
        heights = jax.random.uniform(jax.random.fold_in(jax.random.fold_in(stream_key, 6), axis_at), (parts,), jnp.float32, low / len(split), high / len(split))
        return jnp.repeat(jnp.exp(heights), dims[axis_at] // parts).reshape((-1,) + (1,) * (len(dims) - axis_at - 1))

    level = one(*split[0])
    for cut in split[1:]:
        level = level * one(*cut)
    return level


def shared_out(rng, own, number, rows, count, top, reach, lean):
    ranking = jax.random.permutation(rng, count)
    packed, usual = portions_of(count, rows * top, reach, lean, True), portions_of(count, rows * top, reach, lean, False)
    places = jnp.arange(count)

    def named(tallies, turn):
        used = int((tallies > 0).sum())
        fixed = max(1, used // 4)
        shifted = fixed + (places - fixed + turn * (used - fixed)) % max(1, count - fixed)
        return jnp.zeros((count,), jnp.int32).at[ranking[jnp.where(places < fixed, places, shifted)]].set(jnp.asarray(tallies, jnp.int32))

    tallies = jnp.where(number % 4 == 0, named(packed, number // 4), named(usual, number - number // 4 - 1))
    mixed = jax.random.permutation(jax.random.fold_in(own, 3), count)
    source_of, receiver = mixed[0:count // 2 * 2:2], mixed[1:count // 2 * 2:2]
    room = jnp.minimum(tallies[source_of] - 1, reach - tallies[receiver]) // 2
    room = jnp.where((source_of == ranking[0]) | (receiver == ranking[0]) | (tallies[receiver] == 0), 0, jnp.maximum(room, 0))
    shifted = jax.random.randint(jax.random.fold_in(own, 4), (count // 2,), 0, 1 << 20) % (room + 1)
    tallies = tallies.at[source_of].add(-shifted).at[receiver].add(shifted)
    members = jnp.searchsorted(jnp.cumsum(tallies), jnp.arange(rows * top), side="right").astype(jnp.int32)
    grid = members.reshape(top, rows).T
    grid = grid[jax.random.permutation(jax.random.fold_in(own, 1), rows)]
    turn = jax.random.randint(jax.random.fold_in(own, 2), (rows, 1), 0, top)
    return jnp.take_along_axis(grid, (jnp.arange(top)[None, :] + turn) % top, axis=1)


def portions_of(amount, total, reach, skew, full):
    portions = [(1 << 20) // math.isqrt(rank ** skew) + 1 for rank in range(1, amount + 1)]
    largest = reach if full else min(reach, max(-(-total // amount), total * portions[0] // sum(portions)))
    least = 1 if total - largest >= amount - 1 else 0
    counts, rest = [largest] + [least] * (amount - 1), total - largest - least * (amount - 1)
    while rest > 0:
        movable = [i for i in range(1, amount) if counts[i] < largest] or [i for i in range(1, amount) if counts[i] < reach]
        mass, left = sum([portions[i] for i in movable]), rest
        for i in movable:
            extra = min(reach - counts[i], max(1, left * portions[i] // mass), rest)
            counts[i] = counts[i] + extra
            rest = rest - extra
    return np.array(counts)


def noise(own_key, extent, spread, reach, cuts=(), kind=jnp.bfloat16):
    loudness = steps_of(own_key, extent, cuts, -0.22, 0.18) if cuts else 1.0
    drawn = jax.random.normal(own_key, extent, jnp.float32) * spread * loudness
    return jnp.minimum(jnp.maximum(drawn, -reach), reach).astype(kind)


def setup_inputs(seed: int = 0) -> dict:
    key_of = jax.random.split(jax.random.key(seed), 13)
    section_input = noise(key_of[0], (SECTIONS, TOKENS, D), 1.0, 6.0, ((0, 4), (1, 32)))
    fresh_batch = noise(key_of[1], (TOKENS, D), 1.0, 6.0, ((0, 32),))
    attn_gain = jnp.clip(1.0 + 0.18 * jax.random.normal(key_of[2], (SECTIONS, D), jnp.float32), 0.1, 1.9)
    query_gain = jnp.clip(1.0 + 0.1 * jax.random.normal(key_of[3], (SECTIONS, HEAD), jnp.float32), 0.5, 1.5)
    key_gain = jnp.clip(1.0 + 0.1 * jax.random.normal(key_of[4], (SECTIONS, HEAD), jnp.float32), 0.5, 1.5)
    kv_weight = noise(key_of[5], (SECTIONS, D, 2 * KVH * HEAD), D ** -0.5, 0.125, ((0, 4),))
    out_weight = noise(key_of[6], (SECTIONS, QH * HEAD, D), (QH * HEAD) ** -0.5, 0.125, ((0, 4), (1, 32)))
    moe_gain = jnp.clip(1.0 + 0.18 * jax.random.normal(key_of[7], (SECTIONS, D), jnp.float32), 0.1, 1.9)
    expert_gate_up = noise(key_of[8], (SECTIONS, EXPERTS, D, 2 * FF), D ** -0.5, 0.125, ((0, 4), (1, 32)))
    expert_down = noise(key_of[9], (SECTIONS, EXPERTS, FF, D), FF ** -0.5, 0.21875, ((0, 4), (1, 32)))
    route_ids_keys = jax.random.split(jax.random.fold_in(key_of[10], 1), SECTIONS * 2 * TOKENS // TOK_DEV)
    route_ids_turns = jax.random.permutation(jax.random.fold_in(key_of[10], 3), SECTIONS * 2 * TOKENS // TOK_DEV)
    route_ids = jax.vmap(lambda own, number: shared_out(jax.random.fold_in(key_of[10], 2), own, number, TOK_DEV, EXPERTS, TOPK, CAP, 2))(route_ids_keys, route_ids_turns).reshape((SECTIONS, 2, TOKENS, TOPK))
    route_weights = with_ends(jax.random.randint(key_of[11], (SECTIONS, 2, TOKENS, TOPK), 1, 256), jax.random.fold_in(key_of[11], 1), 1, 255).astype(jnp.int32)
    return dict(section_input=section_input, fresh_batch=fresh_batch, attn_gain=attn_gain, query_gain=query_gain, key_gain=key_gain, kv_weight=kv_weight, out_weight=out_weight, moe_gain=moe_gain, expert_gate_up=expert_gate_up, expert_down=expert_down, route_ids=route_ids, route_weights=route_weights)


EPS = 1e-06

def rms_scale(values, gain):
    mean_sq = lax.optimization_barrier(jnp.mean(values * values, axis=-1, keepdims=True))
    return values * lax.rsqrt(mean_sq + EPS) * gain

def slot_positions(ids, cap, experts_all):
    pairs = ids.shape[0] * ids.shape[1]
    flat = (ids.reshape(pairs, 1) == jnp.arange(experts_all, dtype=jnp.int32)[None, :]).astype(jnp.int32)
    rank = jnp.cumsum(flat, axis=0, dtype=jnp.int32) - flat
    slot = lax.optimization_barrier(jnp.sum(rank * flat, axis=1, dtype=jnp.int32)).reshape(ids.shape)
    return (ids * cap + slot).astype(jnp.int32)

def attention_ref(attn_in, q_gain, k_gain, kv_w):
    tok = attn_in.shape[0]
    kdim = KVH * HEAD
    group = QH // KVH
    kv_raw = jnp.dot(attn_in, kv_w, preferred_element_type=jnp.float32)
    keys = rms_scale(kv_raw[:, :kdim].reshape(tok, KVH, HEAD), k_gain).reshape(tok, kdim)
    keys_values = jnp.concatenate([keys, kv_raw[:, kdim:]], axis=1).astype(jnp.bfloat16)
    queries = (rms_scale(attn_in.astype(jnp.float32).reshape(tok, QH, HEAD), q_gain) * HEAD ** (-0.5)).astype(jnp.bfloat16)
    queries = queries.reshape(tok, KVH, group, HEAD)
    qblock = min(256, SEQ_LEN)

    def one_block(index):
        start = index * qblock
        seq_first = start // SEQ_LEN * SEQ_LEN
        q_rows = lax.dynamic_slice_in_dim(queries, start, qblock, 0).astype(jnp.float32)
        kv_seq = lax.dynamic_slice_in_dim(keys_values, seq_first, SEQ_LEN, 0).astype(jnp.float32)
        key_rows = kv_seq[:, :kdim].reshape(SEQ_LEN, KVH, HEAD)
        value_rows = kv_seq[:, kdim:].reshape(SEQ_LEN, KVH, HEAD)
        scores = jnp.einsum('tkgd,ukd->kgtu', q_rows, key_rows)
        qpos = start + jnp.arange(qblock, dtype=jnp.int32)
        kpos = seq_first + jnp.arange(SEQ_LEN, dtype=jnp.int32)
        allowed = kpos[None, :] <= qpos[:, None]
        expw = jnp.where(allowed, jnp.exp(scores), 0.0)
        total = lax.optimization_barrier(jnp.sum(expw, axis=-1))
        probs = expw.astype(jnp.bfloat16).astype(jnp.float32)
        mixed = jnp.einsum('kgtu,ukd->kgtd', probs, value_rows)
        out = mixed / total[..., None]
        return out.transpose(2, 0, 1, 3).reshape(qblock, QH * HEAD).astype(jnp.bfloat16)
    blocks = lax.map(one_block, jnp.arange(tok // qblock, dtype=jnp.int32))
    return blocks.reshape(tok, QH * HEAD)

def run_expert(args):
    rows, gate_up, down = args
    proj = jnp.dot(rows, gate_up, preferred_element_type=jnp.float32)
    hidden = (jax.nn.silu(proj[:, :FF]) * proj[:, FF:]).astype(jnp.bfloat16)
    return jnp.dot(hidden, down, preferred_element_type=jnp.float32).astype(jnp.bfloat16)

def layer_ref(hidden, a_gain, q_gain, k_gain, kv_w, out_w, m_gain, gate_up, down, ids, weight_ints):
    h32 = hidden.astype(jnp.float32)
    attn_in = rms_scale(h32, a_gain).astype(jnp.bfloat16)
    attended = attention_ref(attn_in, q_gain, k_gain, kv_w)
    after_attn = h32 + jnp.dot(attended, out_w, preferred_element_type=jnp.float32)
    moe_in = rms_scale(after_attn, m_gain).astype(jnp.bfloat16)
    blocks_in = moe_in.reshape(N_EXPERT, TOK_DEV, D)
    ids_blocks = ids.reshape(N_EXPERT, TOK_DEV, TOPK)
    positions = jax.vmap(lambda block_ids: slot_positions(block_ids, CAP, EXPERTS))(ids_blocks)
    token_of_pair = jnp.arange(TOK_DEV * TOPK, dtype=jnp.int32) // TOPK

    def fill(rows, pos):
        buffer = jnp.zeros((EXPERTS * CAP, D), jnp.bfloat16)
        return buffer.at[pos.reshape(-1)].set(rows[token_of_pair])
    buffers = jax.vmap(fill)(blocks_in, positions)
    per_expert = buffers.reshape(N_EXPERT, EXPERTS, CAP, D).transpose(1, 0, 2, 3).reshape(EXPERTS, N_EXPERT * CAP, D)
    outputs = lax.map(run_expert, (per_expert, gate_up, down))
    back = outputs.reshape(EXPERTS, N_EXPERT, CAP, D).transpose(1, 0, 2, 3).reshape(N_EXPERT, EXPERTS * CAP, D)
    picked = jax.vmap(lambda rows, pos: rows[pos])(back, positions)
    gates = weight_ints.astype(jnp.float32).reshape(N_EXPERT, TOK_DEV, TOPK) * (1.0 / 1024.0)
    moe = lax.optimization_barrier(jnp.sum(picked.astype(jnp.float32) * gates[..., None], axis=2)).reshape(TOKENS, D)
    return (after_attn + moe).astype(jnp.bfloat16)

def reference(section_input, fresh_batch, attn_gain, query_gain, key_gain, kv_weight, out_weight, moe_gain, expert_gate_up, expert_down, route_ids, route_weights):

    def apply(section, tick, hidden):
        return layer_ref(hidden, attn_gain[section], query_gain[section], key_gain[section], kv_weight[section], out_weight[section], moe_gain[section], expert_gate_up[section], expert_down[section], route_ids[section, tick], route_weights[section, tick])
    first_list = [apply(section, 0, section_input[section]) for section in range(SECTIONS)]
    second_list = []
    for section in range(SECTIONS):
        incoming = fresh_batch if section == 0 else first_list[section - 1]
        second_list.append(apply(section, 1, incoming))
    return (jnp.stack(first_list), jnp.stack(second_list))
```

```python
import functools
import jax
import jax.numpy as jnp
from jax import lax
from jax.experimental import pallas as pl
from jax.experimental.pallas import tpu as pltpu
from jax.sharding import PartitionSpec as P

HEAD = 64
QH = 32
KVH = 4
TOPK = 8


EPS = 1e-06


def shifted(x, axis, by):
    peers = lax.axis_size(axis)
    pairs = [(i, i + by) for i in range(peers) if 0 <= i + by < peers]
    return lax.ppermute(x, axis, pairs)


def rms_scale(values, gain):
    mean_sq = jnp.mean(values * values, axis=-1, keepdims=True)
    return values * lax.rsqrt(mean_sq + EPS) * gain


def attend(attn_in, q_gain, k_gain, kv_w, place, seq_len):
    tok = attn_in.shape[0]
    kdim = KVH * HEAD
    group = QH // KVH
    kv_raw = jnp.dot(attn_in, kv_w, preferred_element_type=jnp.float32)
    keys = rms_scale(kv_raw[:, :kdim].reshape(tok, KVH, HEAD), k_gain).reshape(tok, kdim)
    keys_values = jnp.concatenate([keys, kv_raw[:, kdim:]], axis=1).astype(jnp.bfloat16)
    queries = (
        rms_scale(attn_in.astype(jnp.float32).reshape(tok, QH, HEAD), q_gain) * HEAD ** (-0.5)
    ).astype(jnp.bfloat16)
    queries = queries.reshape(tok, KVH, group, HEAD)
    first_row = place * tok
    qpos = first_row + jnp.arange(tok, dtype=jnp.int32)
    seq_first = first_row // seq_len * seq_len
    empty = (
        jnp.zeros((KVH, group, tok), jnp.float32),
        jnp.zeros((KVH, group, tok, HEAD), jnp.float32),
    )
    piece = lax.all_gather(keys_values, "expert", axis=0, tiled=True)
    start = jnp.int32(0)
    rows = piece.shape[0]

    def accumulate(state):
        kpos = jnp.arange(rows, dtype=jnp.int32)
        key_rows = piece[:, :kdim].reshape(rows, KVH, HEAD)
        value_rows = piece[:, kdim:].reshape(rows, KVH, HEAD)
        scores = jnp.einsum("tkgd,ukd->kgtu", queries, key_rows, preferred_element_type=jnp.float32)
        allowed = (kpos[None, :] <= qpos[:, None]) & (kpos[None, :] >= seq_first)
        expw = jnp.where(allowed, jnp.exp(scores), 0.0)
        mixed = jnp.einsum(
            "kgtu,ukd->kgtd",
            expw.astype(jnp.bfloat16),
            value_rows,
            preferred_element_type=jnp.float32,
        )
        return (jnp.sum(expw, axis=-1), mixed)

    needed = (start <= qpos[tok - 1]) & (start + rows > seq_first)
    total, mixed = lax.cond(needed, accumulate, lambda state: state, empty)
    out = mixed / total[..., None]
    return out.transpose(2, 0, 1, 3).reshape(tok, QH * HEAD).astype(jnp.bfloat16)


MESH = pl.DeviceIdType.MESH
CHUNKS = 4
BF16 = jnp.bfloat16
F32 = jnp.float32


def route_info(ids, weight_ints, experts_all):
    chosen = ids[:, :, None] == jnp.arange(experts_all, dtype=jnp.int32)[None, None, :]
    member = jnp.any(chosen, axis=1)
    gates = weight_ints.astype(F32) * (1.0 / 1024.0)
    weight = jnp.sum(jnp.where(chosen, gates[..., None], 0.0), axis=1)
    tok = ids.shape[0]
    before = jnp.tril(jnp.ones((tok, tok), BF16), -1)
    rank = jnp.dot(before, member.astype(BF16), preferred_element_type=F32)
    return jnp.concatenate([jnp.where(member, rank, -1.0).T, weight.T], axis=0)


def moe_kernel(
    cap,
    x_ref,
    after_ref,
    info_ref,
    gu_hbm,
    dn_hbm,
    out_ref,
    xg,
    sb,
    xb,
    bb,
    pb,
    pr,
    pf,
    tot,
    infog,
    sel,
    cw,
    ct,
    gu,
    dn,
    acc,
    hid,
    si,
    ri,
    s1,
    r1,
    s2,
    r2,
    s3,
    r3,
    s4,
    r4,
    wsem,
):
    me = lax.axis_index("expert")
    sec = lax.axis_index("section")
    y, z, c = me // 8, (me // 2) % 4, me % 2
    g = c * z + (1 - c) * y
    ln = c * y + (1 - c) * z
    chunks, width = xg.shape[0], xg.shape[3]
    rows = 2 * 4 * cap
    half = 4 * cap
    my_slot = 4 * c + ln
    my_line = 2 * ln + c

    def relay(gp):
        return 2 * (c * (4 * ln + gp) + (1 - c) * (4 * gp + ln)) + c

    def line_dev(i):
        return 2 * (c * (4 * (i // 2) + g) + (1 - c) * (4 * g + i // 2)) + i % 2

    def slot_dev(s):
        t, l0 = s // 4, s % 4
        return (1 - t) * (8 * y + 2 * l0) + t * (8 * l0 + 2 * z + 1)

    def slot_line(s):
        t = s // 4
        return 2 * ((1 - t) * z + t * y) + c

    def remote(src, dst, send, recv, dev):
        return pltpu.make_async_remote_copy(
            src_ref=src,
            dst_ref=dst,
            send_sem=send,
            recv_sem=recv,
            device_id=(sec, dev),
            device_id_type=MESH,
        )

    def info_copy(k):
        gp = (g + k) % 4
        return remote(infog.at[g], infog.at[g], si.at[k], ri.at[g], relay(gp))

    def info_arrival(k):
        gp = (g + k) % 4
        return remote(infog.at[gp], infog.at[gp], si.at[k], ri.at[gp], relay(gp))

    def gather_copy(j, k):
        gp = (g + k) % 4
        return remote(xg.at[j, g], xg.at[j, g], s1.at[j, k], r1.at[j, g], relay(gp))

    def gather_arrival(j, k):
        gp = (g + k) % 4
        return remote(xg.at[j, gp], xg.at[j, gp], s1.at[j, k], r1.at[j, gp], relay(gp))

    def out_copy(j, i):
        return remote(sb.at[j, i], xb.at[j, my_slot], s2.at[j, i], r2.at[j, my_slot], line_dev(i))

    def out_arrival(j, s):
        return remote(xb.at[j, s], xb.at[j, s], s2.at[j, s], r2.at[j, s], slot_dev(s))

    def back_copy(j, s):
        i = slot_line(s)
        return remote(xb.at[j, s], bb.at[j, i], s3.at[j, s], r3.at[j, i], slot_dev(s))

    def back_arrival(j, i):
        return remote(bb.at[j, i], bb.at[j, i], s3.at[j, i], r3.at[j, i], line_dev(i))

    def sum_copy(j, k):
        gp = (g + k) % 4
        return remote(pb.at[j, gp], pr.at[j, g], s4.at[j, k], r4.at[j, g], relay(gp))

    def sum_arrival(j, k):
        gp = (g + k) % 4
        return remote(pr.at[j, gp], pr.at[j, gp], s4.at[j, k], r4.at[j, gp], relay(gp))

    def each(n, first=0):
        def wrap(f):
            def step(i, carry):
                f(i)
                return carry

            lax.fori_loop(first, n, step, 0)

        return wrap

    gu_copy = pltpu.make_async_copy(gu_hbm, gu, wsem.at[0])
    dn_copy = pltpu.make_async_copy(dn_hbm, dn, wsem.at[1])

    barrier = pltpu.get_barrier_semaphore()

    def greet(dev):
        pl.semaphore_signal(barrier, inc=1, device_id=(sec, dev), device_id_type=MESH)

    @each(8, 1)
    def _(k):
        greet(8 * y + (2 * z + c + k) % 8)

    @each(4, 1)
    def _(k):
        greet(8 * ((y + k) % 4) + 2 * z)
        greet(8 * ((y + k) % 4) + 2 * z + 1)

    infog[g] = info_ref[...]
    for j in range(chunks):
        xg[j, g] = x_ref[:, j * width : (j + 1) * width]
    pl.semaphore_wait(barrier, 13)

    @each(4, 1)
    def _(k):
        info_copy(k).start()

    @each(chunks)
    def _(j):
        @each(4, 1)
        def _(k):
            gather_copy(j, k).start()

    gu_copy.start()
    dn_copy.start()
    acc[...] = jnp.zeros_like(acc)

    row = lax.broadcasted_iota(jnp.int32, (half, 512), 0)
    lane = lax.broadcasted_iota(jnp.int32, (half, 512), 1)
    block_of_row = (
        (row >= cap).astype(jnp.int32)
        + (row >= 2 * cap).astype(jnp.int32)
        + (row >= 3 * cap).astype(jnp.int32)
    )
    pattern = jnp.where(block_of_row == lane // 128, row - cap * block_of_row, -5).astype(F32)

    @each(4, 1)
    def _(k):
        info_arrival(k).wait_recv()

    @each(8)
    def _(i):
        dev = line_dev(i)
        picks, gates = [], []
        for e in range(2):
            at = 2 * dev + e
            rank = jnp.concatenate([infog[b, pl.ds(at, 1), :] for b in range(4)], axis=1)
            gate = jnp.concatenate([infog[b, pl.ds(64 + at, 1), :] for b in range(4)], axis=1)
            hit = rank == pattern
            picks.append(jnp.where(hit, 1.0, 0.0))
            gates.append(jnp.where(hit, gate, 0.0))
        at = pl.multiple_of(i * rows, 16)
        sel[pl.ds(at, rows), :] = jnp.concatenate(picks, axis=0).astype(BF16)
        cw[pl.ds(at, rows), :] = jnp.concatenate(gates, axis=0).astype(BF16)

    @each(chunks)
    def _(j):
        @each(4, 1)
        def _(k):
            gather_arrival(j, k).wait_recv()

        @each(width // 256)
        def _(n):
            cols = pl.ds(pl.multiple_of(n * 256, 256), 256)
            held = xg[j, :, :, cols].reshape(512, 256)
            got = jnp.dot(sel[...], held, preferred_element_type=F32)
            sb[j, :, :, cols] = got.astype(BF16).reshape(8, rows, 256)

        @each(8, 1)
        def _(k):
            out_copy(j, (my_line + k) % 8).start()

        xb[j, my_slot] = sb[j, my_line]

    for m in range(8 * rows // 128):
        ct[:, m * 128 : (m + 1) * 128] = (
            cw[m * 128 : (m + 1) * 128, :].astype(F32).T.astype(BF16)
        )

    gu_copy.wait()

    @each(chunks)
    def _(j):
        @each(8, 1)
        def _(k):
            out_arrival(j, (my_slot + k) % 8).wait_recv()

        for e in range(2):
            first = e * (rows - 80)

            @each(acc.shape[2] // 256)
            def _(n):
                cols = pl.ds(pl.multiple_of(n * 256, 256), 256)
                lhs = xb[j, :, first : first + 80, :].reshape(640, width)
                rhs = gu[e, pl.ds(pl.multiple_of(j * width, width), width), cols]
                acc[e, :, cols] += jnp.dot(lhs, rhs, preferred_element_type=F32)

    ff = hid.shape[2]
    for e in range(2):

        @each(640 // 128)
        def _(m):
            at = pl.ds(pl.multiple_of(m * 128, 128), 128)
            hid[e, at, :] = (jax.nn.silu(acc[e, at, :ff]) * acc[e, at, ff:]).astype(BF16)

    dn_copy.wait()

    @each(chunks)
    def _(j):
        @each(width // 256)
        def _(n):
            cols = pl.ds(pl.multiple_of(n * 256, 256), 256)
            at = pl.ds(pl.multiple_of(j * width + n * 256, 256), 256)
            made = [
                jnp.dot(hid[e], dn[e, :, at], preferred_element_type=F32).reshape(8, 80, 256)
                for e in range(2)
            ]
            line = lax.broadcasted_iota(jnp.int32, (8, 16, 256), 1)
            shared = jnp.where(line < 8, made[0][:, 64:80], made[1][:, 0:16])
            xb[j, :, 0:64, cols] = made[0][:, 0:64].astype(BF16)
            xb[j, :, 64:80, cols] = shared.astype(BF16)
            xb[j, :, 80:144, cols] = made[1][:, 16:80].astype(BF16)

        @each(8, 1)
        def _(k):
            back_copy(j, (my_slot + k) % 8).start()

        bb[j, my_line] = xb[j, my_slot]

    @each(chunks)
    def _(j):
        @each(8, 1)
        def _(k):
            back_arrival(j, (my_line + k) % 8).wait_recv()

        @each(width // 256)
        def _(n):
            cols = pl.ds(pl.multiple_of(n * 256, 256), 256)
            at = pl.ds(pl.multiple_of(j * width + n * 256, 256), 256)
            part = jnp.dot(
                ct[...], bb[j, :, :, cols].reshape(8 * rows, 256), preferred_element_type=F32
            ).reshape(4, 128, 256)
            pf[...] = part
            pb[j, :, :, cols] = part.astype(BF16)
            tot[:, at] = after_ref[:, at] + pf[g]

        @each(4, 1)
        def _(k):
            sum_copy(j, k).start()

    @each(chunks)
    def _(j):
        at = pl.ds(pl.multiple_of(j * width, width), width)

        @each(4, 1)
        def _(k):
            sum_arrival(j, k).wait_recv()
            tot[:, at] += pr[j, (g + k) % 4].astype(F32)

        out_ref[:, at] = tot[:, at].astype(BF16)

    @each(4, 1)
    def _(k):
        info_copy(k).wait_send()

    @each(chunks)
    def _(j):
        @each(4, 1)
        def _(k):
            gather_copy(j, k).wait_send()
            sum_copy(j, k).wait_send()

        @each(8, 1)
        def _(k):
            out_copy(j, (my_line + k) % 8).wait_send()
            back_copy(j, (my_slot + k) % 8).wait_send()


def moe_layer(moe_in, after_attn, info, gate_up, down, cap, tick):
    tok, d = moe_in.shape
    ff = down.shape[1]
    w = d // CHUNKS
    rows = 8 * cap
    vmem = pl.BlockSpec(memory_space=pltpu.VMEM)
    hbm = pl.BlockSpec(memory_space=pl.ANY)
    dma = pltpu.SemaphoreType.DMA
    return pl.pallas_call(
        functools.partial(moe_kernel, cap),
        out_shape=jax.ShapeDtypeStruct((tok, d), BF16),
        in_specs=[vmem, vmem, vmem, hbm, hbm],
        out_specs=vmem,
        scratch_shapes=[
            pltpu.VMEM((CHUNKS, 4, tok, w), BF16),
            pltpu.VMEM((CHUNKS, 8, rows, w), BF16),
            pltpu.VMEM((CHUNKS, 8, rows, w), BF16),
            pltpu.VMEM((CHUNKS, 8, rows, w), BF16),
            pltpu.VMEM((CHUNKS, 4, tok, w), BF16),
            pltpu.VMEM((CHUNKS, 4, tok, w), BF16),
            pltpu.VMEM((4, tok, 256), F32),
            pltpu.VMEM((tok, d), F32),
            pltpu.VMEM((4, 128, tok), F32),
            pltpu.VMEM((8 * rows, 4 * tok), BF16),
            pltpu.VMEM((8 * rows, 4 * tok), BF16),
            pltpu.VMEM((4 * tok, 8 * rows), BF16),
            pltpu.VMEM(gate_up.shape, BF16),
            pltpu.VMEM(down.shape, BF16),
            pltpu.VMEM((2, 640, 2 * ff), F32),
            pltpu.VMEM((2, 640, ff), BF16),
            dma((4,)),
            dma((4,)),
            dma((CHUNKS, 4)),
            dma((CHUNKS, 4)),
            dma((CHUNKS, 8)),
            dma((CHUNKS, 8)),
            dma((CHUNKS, 8)),
            dma((CHUNKS, 8)),
            dma((CHUNKS, 4)),
            dma((CHUNKS, 4)),
            dma((2,)),
        ],
        compiler_params=pltpu.CompilerParams(
            collective_id=4 + tick, has_side_effects=True, vmem_limit_bytes=64 << 20
        ),
        cost_estimate=pl.CostEstimate(
            flops=12 * 10**9, bytes_accessed=20 * 10**6, transcendentals=10**6
        ),
    )(moe_in, after_attn, info, gate_up, down)


def body(
    section_input,
    fresh_batch,
    attn_gain,
    query_gain,
    key_gain,
    kv_weight,
    out_weight,
    moe_gain,
    expert_gate_up,
    expert_down,
    route_ids,
    route_weights,
):
    devices = lax.axis_size("expert")
    place = lax.axis_index("expert")
    tok = section_input.shape[1]
    experts_all = expert_gate_up.shape[1] * devices
    cap = tok * TOPK * 9 // (8 * experts_all)
    seq_len = tok * devices
    infos = [route_info(route_ids[0, t], route_weights[0, t], experts_all) for t in range(2)]
    out_full = lax.all_gather(out_weight[0], "expert", axis=0, tiled=True)

    def layer(hidden, tick):
        h32 = hidden.astype(jnp.float32)
        attn_in = rms_scale(h32, attn_gain[0]).astype(jnp.bfloat16)
        attended = attend(attn_in, query_gain[0], key_gain[0], kv_weight[0], place, seq_len)
        after_attn = h32 + jnp.dot(attended, out_full, preferred_element_type=jnp.float32)
        moe_in = rms_scale(after_attn, moe_gain[0]).astype(jnp.bfloat16)
        return moe_layer(
            moe_in, after_attn, infos[tick], expert_gate_up[0], expert_down[0], cap, tick
        )

    first_out = layer(section_input[0], 0)
    incoming = shifted(first_out, "section", 1)
    second_in = jnp.where(lax.axis_index("section") == 0, fresh_batch, incoming)
    second_out = layer(second_in, 1)
    return (first_out[None], second_out[None])


def solution(mesh):
    in_specs = (
        P("section", "expert", None),
        P("expert", None),
        P("section", None),
        P("section", None),
        P("section", None),
        P("section", None, None),
        P("section", "expert", None),
        P("section", None),
        P("section", "expert", None, None),
        P("section", "expert", None, None),
        P("section", None, "expert", None),
        P("section", None, "expert", None),
    )
    out_specs = (P("section", "expert", None), P("section", "expert", None))
    return jax.shard_map(body, mesh=mesh, in_specs=in_specs, out_specs=out_specs, check_vma=False)
```

```python
import functools
import math

import jax
import jax.numpy as jnp
from jax import lax
from jax.experimental import pallas as pl
from jax.experimental.pallas import tpu as pltpu
from jax.sharding import PartitionSpec as P

HEAD = 64
QH = 32
KVH = 4
TOPK = 8
EPS = 1e-06
MESH = pl.DeviceIdType.MESH
CHUNKS = 4
BF16 = jnp.bfloat16
F32 = jnp.float32


def each(n, first=0):
    def wrap(f):
        def step(i, carry):
            f(i)
            return carry

        lax.fori_loop(first, n, step, 0)

    return wrap


def route_info(ids, weight_ints, experts_all):
    chosen = ids[:, :, None] == jnp.arange(experts_all, dtype=jnp.int32)[None, None, :]
    member = jnp.any(chosen, axis=1)
    gates = weight_ints.astype(F32) * (1.0 / 1024.0)
    weight = jnp.sum(jnp.where(chosen, gates[..., None], 0.0), axis=1)
    tok = ids.shape[0]
    before = jnp.tril(jnp.ones((tok, tok), BF16), -1)
    rank = jnp.dot(before, member.astype(BF16), preferred_element_type=F32)
    return jnp.concatenate([jnp.where(member, rank, -1.0).T, weight.T], axis=0)


def rms_scale(values, gain):
    mean_sq = jnp.mean(values * values, axis=-1, keepdims=True)
    return values * lax.rsqrt(mean_sq + EPS) * gain


def attn_kernel(
    h_ref, gain_ref, qgain_ref, kgain_ref, kvw_ref, out_ref, kv, qs, acc, s1, s2, s3, rk
):
    me = lax.axis_index("expert")
    sec = lax.axis_index("section")
    y, z, c = me // 8, (me // 2) % 4, me % 2
    g = c * z + (1 - c) * y
    ln = c * y + (1 - c) * z
    tok = h_ref.shape[0]
    kdim = KVH * HEAD
    group = QH // KVH

    def peer(gp, lp):
        return 2 * (c * (4 * lp + gp) + (1 - c) * (4 * gp + lp)) + c

    sibling = me + 1 - 2 * c

    def remote(block, send, dev):
        return pltpu.make_async_remote_copy(
            src_ref=kv.at[block],
            dst_ref=kv.at[block],
            send_sem=send,
            recv_sem=rk.at[block],
            device_id=(sec, dev),
            device_id_type=MESH,
        )

    def gather_copy(k):
        return remote(me, s1.at[k], peer((g + k) % 4, ln))

    def line_copy(gp, k):
        return remote(peer(gp, ln), s2.at[4 * gp + k], peer(g, (ln + k) % 4))

    def pair_copy(gp, lp):
        return remote(peer(gp, lp), s3.at[4 * gp + lp], sibling)

    def arrival(block):
        return remote(block, s1.at[0], sibling)

    barrier = pltpu.get_barrier_semaphore()

    def greet(dev):
        pl.semaphore_signal(barrier, inc=1, device_id=(sec, dev), device_id_type=MESH)

    @each(4, 1)
    def _(k):
        greet(peer((g + k) % 4, ln))
        greet(peer(g, (ln + k) % 4))

    greet(sibling)

    r0 = lax.broadcasted_iota(jnp.int32, (256, 256), 0) // HEAD
    c0 = lax.broadcasted_iota(jnp.int32, (256, 256), 1) // HEAD
    averager = jnp.where(r0 == c0, 1.0 / HEAD, 0.0).astype(BF16)

    def head_means(x):
        sq = x * x
        high = sq.astype(BF16)
        low = (sq - high.astype(F32)).astype(BF16)
        return jnp.dot(high, averager, preferred_element_type=F32) + jnp.dot(
            low, averager, preferred_element_type=F32
        )

    h32 = h_ref[...].astype(F32)
    scale = lax.rsqrt(jnp.mean(h32 * h32, axis=-1, keepdims=True) + EPS)
    attn_in = (h32 * scale * gain_ref[...]).astype(BF16)
    kv_raw = jnp.dot(attn_in, kvw_ref[...], preferred_element_type=F32)
    keys = kv_raw[:, :kdim]
    keys = keys * lax.rsqrt(head_means(keys) + EPS) * kgain_ref[...]
    kv[me] = jnp.concatenate([keys, kv_raw[:, kdim:]], axis=1).astype(BF16)

    pl.semaphore_wait(barrier, 7)

    @each(4, 1)
    def _(k):
        gather_copy(k).start()

    @each(4, 1)
    def _(k):
        line_copy(g, k).start()

    pair_copy(g, ln).start()

    low_half = lax.broadcasted_iota(jnp.int32, (tok, 128), 1) < HEAD
    for t in range(QH * HEAD // 256):
        part = attn_in[:, 256 * t : 256 * t + 256].astype(F32)
        query = part * lax.rsqrt(head_means(part) + EPS) * qgain_ref[:, 256 * t : 256 * t + 256]
        for n in range(4):
            head = 4 * t + n
            at = (head // group) % 2
            tile = query[:, 128 * (n // 2) : 128 * (n // 2) + 128]
            if n % 2 != at:
                tile = pltpu.roll(tile, HEAD, 1)
            tile = jnp.where(low_half == (at == 0), tile, 0.0)
            first = head % group * tok
            qs[head // group, first : first + tok, :] = tile.astype(BF16)

    @each(4, 1)
    def _(k):
        gp = (g + k) % 4
        arrival(peer(gp, ln)).wait_recv()

        @each(4, 1)
        def _(m):
            line_copy(gp, m).start()

        pair_copy(gp, ln).start()

    @each(4)
    def _(m):
        gp = (g + m) % 4

        @each(4, 1)
        def _(k):
            lp = (ln + k) % 4
            arrival(peer(gp, lp)).wait_recv()
            pair_copy(gp, lp).start()

    @each(16)
    def _(n):
        arrival(2 * n + 1 - c).wait_recv()

    span = 4 * tok
    ones = jnp.ones((span, 128), BF16)
    last = me // 4
    rows = group * tok
    qpos = me * tok + lax.broadcasted_iota(jnp.int32, (rows, span), 0) % tok
    upos = lax.broadcasted_iota(jnp.int32, (rows, span), 1)

    @each(KVH // 2)
    def _(pair):
        kcols = pl.ds(pl.multiple_of(pair * 128, 128), 128)
        vcols = pl.ds(pl.multiple_of(kdim + pair * 128, 128), 128)
        for at in range(2):

            def step(kb, masked):
                keys = kv[pl.ds(4 * kb, 4), :, kcols].reshape(span, 128)
                values = kv[pl.ds(4 * kb, 4), :, vcols].reshape(span, 128)
                score = lax.dot_general(
                    qs[2 * pair + at],
                    keys,
                    (((1,), (1,)), ((), ())),
                    preferred_element_type=F32,
                )
                expw = jnp.exp2(score)
                if masked:
                    expw = jnp.where(upos + kb * span <= qpos, expw, 0.0)
                return jnp.dot(
                    expw.astype(BF16),
                    jnp.concatenate([values, ones], axis=1),
                    preferred_element_type=F32,
                )

            acc[...] = step(last, True)

            def body(kb, carry):
                acc[...] += step(kb, False)
                return carry

            lax.fori_loop(0, last, body, 0)
            mixed = acc[:, :128] / acc[:, 128:]
            for n in range(group // 2):
                even = mixed[2 * n * tok : (2 * n + 1) * tok]
                odd = mixed[(2 * n + 1) * tok : (2 * n + 2) * tok]
                if at == 0:
                    odd = pltpu.roll(odd, HEAD, 1)
                else:
                    even = pltpu.roll(even, HEAD, 1)
                first = pl.multiple_of((2 * pair + at) * (group // 2) * 128 + n * 128, 128)
                out_ref[:, pl.ds(first, 128)] = jnp.where(low_half, even, odd).astype(BF16)

    @each(4, 1)
    def _(k):
        gather_copy(k).wait_send()

    @each(4)
    def _(gp):
        @each(4, 1)
        def _(k):
            line_copy(gp, k).wait_send()

        @each(4)
        def _(lp):
            pair_copy(gp, lp).wait_send()


def attend(hidden, attn_gain, q_gain, k_gain, kv_w, tick):
    tok, d = hidden.shape
    vmem = pl.BlockSpec(memory_space=pltpu.VMEM)
    dma = pltpu.SemaphoreType.DMA
    qscale = jnp.tile(q_gain * (HEAD**-0.5 * math.log2(math.e)), QH)[None]
    return pl.pallas_call(
        attn_kernel,
        out_shape=jax.ShapeDtypeStruct((tok, d), BF16),
        in_specs=[vmem] * 5,
        out_specs=vmem,
        scratch_shapes=[
            pltpu.VMEM((32, tok, 2 * KVH * HEAD), BF16),
            pltpu.VMEM((KVH, QH // KVH * tok, 128), BF16),
            pltpu.VMEM((QH // KVH * tok, 256), F32),
            dma((4,)),
            dma((16,)),
            dma((16,)),
            dma((32,)),
        ],
        compiler_params=pltpu.CompilerParams(
            collective_id=2 + tick, has_side_effects=True, vmem_limit_bytes=56 << 20
        ),
        cost_estimate=pl.CostEstimate(
            flops=40 * 10**9, bytes_accessed=20 * 10**6, transcendentals=10**6
        ),
    )(hidden, attn_gain[None], qscale, jnp.tile(k_gain, KVH)[None], kv_w)


def moe_kernel(
    cap,
    passes,
    *refs,
):
    if passes:
        x_ref, after_ref, info_ref, gu_hbm, dn_hbm, fresh_ref, out_ref, next_ref = refs[:8]
        ob, nb, s5, r5 = refs[-4:]
        refs = refs[8:-4]
    else:
        x_ref, after_ref, info_ref, gu_hbm, dn_hbm, out_ref = refs[:6]
        refs = refs[6:]
    (
    xg,
    sb,
    xb,
    bb,
    pb,
    pr,
    pf,
    tot,
    infog,
    sel,
    cw,
    ct,
    gu,
    dn,
    acc,
    hid,
    si,
    ri,
    s1,
    r1,
    s2,
    r2,
    s3,
    r3,
    s4,
    r4,
    wsem,
    ) = refs
    me = lax.axis_index("expert")
    sec = lax.axis_index("section")
    y, z, c = me // 8, (me // 2) % 4, me % 2
    g = c * z + (1 - c) * y
    ln = c * y + (1 - c) * z
    chunks, width = xg.shape[0], xg.shape[3]
    rows = 2 * 4 * cap
    half = 4 * cap
    my_slot = 4 * c + ln
    my_line = 2 * ln + c

    def relay(gp):
        return 2 * (c * (4 * ln + gp) + (1 - c) * (4 * gp + ln)) + c

    def line_dev(i):
        return 2 * (c * (4 * (i // 2) + g) + (1 - c) * (4 * g + i // 2)) + i % 2

    def slot_dev(s):
        t, l0 = s // 4, s % 4
        return (1 - t) * (8 * y + 2 * l0) + t * (8 * l0 + 2 * z + 1)

    def slot_line(s):
        t = s // 4
        return 2 * ((1 - t) * z + t * y) + c

    def remote(src, dst, send, recv, dev):
        return pltpu.make_async_remote_copy(
            src_ref=src,
            dst_ref=dst,
            send_sem=send,
            recv_sem=recv,
            device_id=(sec, dev),
            device_id_type=MESH,
        )

    def info_copy(k):
        gp = (g + k) % 4
        return remote(infog.at[g], infog.at[g], si.at[k], ri.at[g], relay(gp))

    def info_arrival(k):
        gp = (g + k) % 4
        return remote(infog.at[gp], infog.at[gp], si.at[k], ri.at[gp], relay(gp))

    def gather_copy(j, k):
        gp = (g + k) % 4
        return remote(xg.at[j, g], xg.at[j, g], s1.at[j, k], r1.at[j, g], relay(gp))

    def gather_arrival(j, k):
        gp = (g + k) % 4
        return remote(xg.at[j, gp], xg.at[j, gp], s1.at[j, k], r1.at[j, gp], relay(gp))

    def out_copy(j, i):
        return remote(sb.at[j, i], xb.at[j, my_slot], s2.at[j, i], r2.at[j, my_slot], line_dev(i))

    def out_arrival(j, s):
        return remote(xb.at[j, s], xb.at[j, s], s2.at[j, s], r2.at[j, s], slot_dev(s))

    def back_copy(j, s):
        i = slot_line(s)
        return remote(xb.at[j, s], bb.at[j, i], s3.at[j, s], r3.at[j, i], slot_dev(s))

    def back_arrival(j, i):
        return remote(bb.at[j, i], bb.at[j, i], s3.at[j, i], r3.at[j, i], line_dev(i))

    def sum_copy(j, k):
        gp = (g + k) % 4
        return remote(pb.at[j, gp], pr.at[j, g], s4.at[j, k], r4.at[j, g], relay(gp))

    def sum_arrival(j, k):
        gp = (g + k) % 4
        return remote(pr.at[j, gp], pr.at[j, gp], s4.at[j, k], r4.at[j, gp], relay(gp))

    def next_copy(j):
        return pltpu.make_async_remote_copy(
            src_ref=ob.at[j],
            dst_ref=nb.at[j],
            send_sem=s5.at[j],
            recv_sem=r5.at[j],
            device_id=((sec + 1) % 4, me),
            device_id_type=MESH,
        )

    gu_copy = pltpu.make_async_copy(gu_hbm, gu, wsem.at[0])
    dn_copy = pltpu.make_async_copy(dn_hbm, dn, wsem.at[1])

    barrier = pltpu.get_barrier_semaphore()

    def greet(dev):
        pl.semaphore_signal(barrier, inc=1, device_id=(sec, dev), device_id_type=MESH)

    @each(8, 1)
    def _(k):
        greet(8 * y + (2 * z + c + k) % 8)

    @each(4, 1)
    def _(k):
        greet(8 * ((y + k) % 4) + 2 * z)
        greet(8 * ((y + k) % 4) + 2 * z + 1)

    if passes:
        for by in (1, 3):
            pl.semaphore_signal(
                barrier, inc=1, device_id=((sec + by) % 4, me), device_id_type=MESH
            )

    infog[g] = info_ref[...]
    for j in range(chunks):
        xg[j, g] = x_ref[:, j * width : (j + 1) * width]
    pl.semaphore_wait(barrier, 15 if passes else 13)

    @each(4, 1)
    def _(k):
        info_copy(k).start()

    @each(chunks)
    def _(j):
        @each(4, 1)
        def _(k):
            gather_copy(j, k).start()

    gu_copy.start()
    dn_copy.start()
    acc[...] = jnp.zeros_like(acc)

    row = lax.broadcasted_iota(jnp.int32, (half, 512), 0)
    lane = lax.broadcasted_iota(jnp.int32, (half, 512), 1)
    block_of_row = (
        (row >= cap).astype(jnp.int32)
        + (row >= 2 * cap).astype(jnp.int32)
        + (row >= 3 * cap).astype(jnp.int32)
    )
    pattern = jnp.where(block_of_row == lane // 128, row - cap * block_of_row, -5).astype(F32)

    @each(4, 1)
    def _(k):
        info_arrival(k).wait_recv()

    @each(8)
    def _(i):
        dev = line_dev(i)
        picks, gates = [], []
        for e in range(2):
            at = 2 * dev + e
            rank = jnp.concatenate([infog[b, pl.ds(at, 1), :] for b in range(4)], axis=1)
            gate = jnp.concatenate([infog[b, pl.ds(64 + at, 1), :] for b in range(4)], axis=1)
            hit = rank == pattern
            picks.append(jnp.where(hit, 1.0, 0.0))
            gates.append(jnp.where(hit, gate, 0.0))
        at = pl.multiple_of(i * rows, 16)
        sel[pl.ds(at, rows), :] = jnp.concatenate(picks, axis=0).astype(BF16)
        cw[pl.ds(at, rows), :] = jnp.concatenate(gates, axis=0).astype(BF16)

    @each(chunks)
    def _(j):
        @each(4, 1)
        def _(k):
            gather_arrival(j, k).wait_recv()

        @each(width // 256)
        def _(n):
            cols = pl.ds(pl.multiple_of(n * 256, 256), 256)
            held = xg[j, :, :, cols].reshape(512, 256)
            got = jnp.dot(sel[...], held, preferred_element_type=F32)
            sb[j, :, :, cols] = got.astype(BF16).reshape(8, rows, 256)

        @each(8, 1)
        def _(k):
            out_copy(j, (my_line + k) % 8).start()

        xb[j, my_slot] = sb[j, my_line]

    for m in range(8 * rows // 128):
        ct[:, m * 128 : (m + 1) * 128] = (
            cw[m * 128 : (m + 1) * 128, :].astype(F32).T.astype(BF16)
        )

    gu_copy.wait()

    @each(chunks)
    def _(j):
        @each(8, 1)
        def _(k):
            out_arrival(j, (my_slot + k) % 8).wait_recv()

        for e in range(2):
            first = e * (rows - 80)

            @each(acc.shape[2] // 256)
            def _(n):
                cols = pl.ds(pl.multiple_of(n * 256, 256), 256)
                lhs = xb[j, :, first : first + 80, :].reshape(640, width)
                rhs = gu[e, pl.ds(pl.multiple_of(j * width, width), width), cols]
                acc[e, :, cols] += jnp.dot(lhs, rhs, preferred_element_type=F32)

    ff = hid.shape[2]
    for e in range(2):

        @each(640 // 128)
        def _(m):
            at = pl.ds(pl.multiple_of(m * 128, 128), 128)
            hid[e, at, :] = (jax.nn.silu(acc[e, at, :ff]) * acc[e, at, ff:]).astype(BF16)

    dn_copy.wait()

    @each(chunks)
    def _(j):
        @each(width // 256)
        def _(n):
            cols = pl.ds(pl.multiple_of(n * 256, 256), 256)
            at = pl.ds(pl.multiple_of(j * width + n * 256, 256), 256)
            made = [
                jnp.dot(hid[e], dn[e, :, at], preferred_element_type=F32).reshape(8, 80, 256)
                for e in range(2)
            ]
            line = lax.broadcasted_iota(jnp.int32, (8, 16, 256), 1)
            shared = jnp.where(line < 8, made[0][:, 64:80], made[1][:, 0:16])
            xb[j, :, 0:64, cols] = made[0][:, 0:64].astype(BF16)
            xb[j, :, 64:80, cols] = shared.astype(BF16)
            xb[j, :, 80:144, cols] = made[1][:, 16:80].astype(BF16)

        @each(8, 1)
        def _(k):
            back_copy(j, (my_slot + k) % 8).start()

        bb[j, my_line] = xb[j, my_slot]

    @each(chunks)
    def _(j):
        @each(8, 1)
        def _(k):
            back_arrival(j, (my_line + k) % 8).wait_recv()

        @each(width // 256)
        def _(n):
            cols = pl.ds(pl.multiple_of(n * 256, 256), 256)
            at = pl.ds(pl.multiple_of(j * width + n * 256, 256), 256)
            part = jnp.dot(
                ct[...], bb[j, :, :, cols].reshape(8 * rows, 256), preferred_element_type=F32
            ).reshape(4, 128, 256)
            pf[...] = part
            pb[j, :, :, cols] = part.astype(BF16)
            tot[:, at] = after_ref[:, at] + pf[g]

        @each(4, 1)
        def _(k):
            sum_copy(j, k).start()

    @each(chunks)
    def _(j):
        at = pl.ds(pl.multiple_of(j * width, width), width)

        @each(4, 1)
        def _(k):
            sum_arrival(j, k).wait_recv()
            tot[:, at] += pr[j, (g + k) % 4].astype(F32)

        made = tot[:, at].astype(BF16)
        out_ref[:, at] = made
        if passes:
            ob[j] = made
            next_copy(j).start()

    if passes:

        @each(chunks)
        def _(j):
            at = pl.ds(pl.multiple_of(j * width, width), width)
            next_copy(j).wait()
            next_ref[:, at] = jnp.where(sec == 0, fresh_ref[:, at], nb[j])

    @each(4, 1)
    def _(k):
        info_copy(k).wait_send()

    @each(chunks)
    def _(j):
        @each(4, 1)
        def _(k):
            gather_copy(j, k).wait_send()
            sum_copy(j, k).wait_send()

        @each(8, 1)
        def _(k):
            out_copy(j, (my_line + k) % 8).wait_send()
            back_copy(j, (my_slot + k) % 8).wait_send()


def moe_layer(moe_in, after_attn, info, gate_up, down, cap, tick, fresh):
    tok, d = moe_in.shape
    ff = down.shape[1]
    w = d // CHUNKS
    rows = 8 * cap
    vmem = pl.BlockSpec(memory_space=pltpu.VMEM)
    hbm = pl.BlockSpec(memory_space=pl.ANY)
    dma = pltpu.SemaphoreType.DMA
    passes = fresh is not None
    outs = 2 if passes else 1
    handed = [
        pltpu.VMEM((CHUNKS, tok, w), BF16),
        pltpu.VMEM((CHUNKS, tok, w), BF16),
        dma((CHUNKS,)),
        dma((CHUNKS,)),
    ]
    return pl.pallas_call(
        functools.partial(moe_kernel, cap, passes),
        out_shape=[jax.ShapeDtypeStruct((tok, d), BF16)] * outs,
        in_specs=[vmem, vmem, vmem, hbm, hbm] + [vmem] * passes,
        out_specs=[vmem] * outs,
        scratch_shapes=[
            pltpu.VMEM((CHUNKS, 4, tok, w), BF16),
            pltpu.VMEM((CHUNKS, 8, rows, w), BF16),
            pltpu.VMEM((CHUNKS, 8, rows, w), BF16),
            pltpu.VMEM((CHUNKS, 8, rows, w), BF16),
            pltpu.VMEM((CHUNKS, 4, tok, w), BF16),
            pltpu.VMEM((CHUNKS, 4, tok, w), BF16),
            pltpu.VMEM((4, tok, 256), F32),
            pltpu.VMEM((tok, d), F32),
            pltpu.VMEM((4, 128, tok), F32),
            pltpu.VMEM((8 * rows, 4 * tok), BF16),
            pltpu.VMEM((8 * rows, 4 * tok), BF16),
            pltpu.VMEM((4 * tok, 8 * rows), BF16),
            pltpu.VMEM(gate_up.shape, BF16),
            pltpu.VMEM(down.shape, BF16),
            pltpu.VMEM((2, 640, 2 * ff), F32),
            pltpu.VMEM((2, 640, ff), BF16),
            dma((4,)),
            dma((4,)),
            dma((CHUNKS, 4)),
            dma((CHUNKS, 4)),
            dma((CHUNKS, 8)),
            dma((CHUNKS, 8)),
            dma((CHUNKS, 8)),
            dma((CHUNKS, 8)),
            dma((CHUNKS, 4)),
            dma((CHUNKS, 4)),
            dma((2,)),
        ]
        + handed * passes,
        compiler_params=pltpu.CompilerParams(
            collective_id=4 + tick, has_side_effects=True, vmem_limit_bytes=64 << 20
        ),
        cost_estimate=pl.CostEstimate(
            flops=12 * 10**9, bytes_accessed=20 * 10**6, transcendentals=10**6
        ),
    )(moe_in, after_attn, info, gate_up, down, *([fresh] if passes else []))


def body(
    section_input,
    fresh_batch,
    attn_gain,
    query_gain,
    key_gain,
    kv_weight,
    out_weight,
    moe_gain,
    expert_gate_up,
    expert_down,
    route_ids,
    route_weights,
):
    devices = lax.axis_size("expert")
    tok = section_input.shape[1]
    experts_all = expert_gate_up.shape[1] * devices
    cap = tok * TOPK * 9 // (8 * experts_all)
    infos = [route_info(route_ids[0, t], route_weights[0, t], experts_all) for t in range(2)]
    out_full = lax.all_gather(out_weight[0], "expert", axis=0, tiled=True)

    def layer(hidden, tick, fresh):
        h32 = hidden.astype(F32)
        attended = attend(hidden, attn_gain[0], query_gain[0], key_gain[0], kv_weight[0], tick)
        after_attn = h32 + jnp.dot(attended, out_full, preferred_element_type=F32)
        moe_in = rms_scale(after_attn, moe_gain[0]).astype(BF16)
        return moe_layer(
            moe_in, after_attn, infos[tick], expert_gate_up[0], expert_down[0], cap, tick, fresh
        )

    first_out, second_in = layer(section_input[0], 0, fresh_batch)
    (second_out,) = layer(second_in, 1, None)
    return (first_out[None], second_out[None])


def solution(mesh):
    in_specs = (
        P("section", "expert", None),
        P("expert", None),
        P("section", None),
        P("section", None),
        P("section", None),
        P("section", None, None),
        P("section", "expert", None),
        P("section", None),
        P("section", "expert", None, None),
        P("section", "expert", None, None),
        P("section", None, "expert", None),
        P("section", None, "expert", None),
    )
    out_specs = (P("section", "expert", None), P("section", "expert", None))
    return jax.shard_map(body, mesh=mesh, in_specs=in_specs, out_specs=out_specs, check_vma=False)
```

```python
import functools
import math

import jax
import jax.numpy as jnp
from jax import lax
from jax.experimental import pallas as pl
from jax.experimental.pallas import tpu as pltpu
from jax.sharding import PartitionSpec as P

HEAD = 64
QH = 32
KVH = 4
TOPK = 8
EPS = 1e-06
MESH = pl.DeviceIdType.MESH
CHUNKS = 4
BF16 = jnp.bfloat16
F32 = jnp.float32


def each(n, first=0):
    def wrap(f):
        def step(i, carry):
            f(i)
            return carry

        lax.fori_loop(first, n, step, 0)

    return wrap


def route_info(ids, gates, experts_all):
    topk, tok = ids.shape
    expert = lax.broadcasted_iota(jnp.int32, (experts_all, tok), 0)
    member = jnp.zeros((experts_all, tok), F32)
    weight = jnp.zeros((experts_all, tok), F32)
    for k in range(topk):
        chosen = ids[k : k + 1] == expert
        member += jnp.where(chosen, 1.0, 0.0)
        weight += jnp.where(chosen, gates[k : k + 1], 0.0)
    earlier = lax.broadcasted_iota(jnp.int32, (tok, tok), 0)
    later = lax.broadcasted_iota(jnp.int32, (tok, tok), 1)
    before = jnp.where(earlier < later, 1.0, 0.0).astype(BF16)
    rank = jnp.dot(member.astype(BF16), before, preferred_element_type=F32)
    return jnp.concatenate([jnp.where(member > 0.5, rank, -1.0), weight], axis=0)


def silu(x):
    half = 0.5 * x
    return half + half * jnp.tanh(half)


class Exchange:
    def __init__(self, buf, s1, s2, sf, s3, rk, sec, c, g, ln, sibling):
        self.buf, self.s1, self.s2, self.sf, self.s3, self.rk = buf, s1, s2, sf, s3, rk
        self.sec, self.c, self.g, self.ln, self.sibling = sec, c, g, ln, sibling

    def slot(self, t, lp, gp):
        return (t * 4 + lp) * 4 + gp

    def peer(self, lp, gp):
        c = self.c
        return 2 * (c * (4 * lp + gp) + (1 - c) * (4 * gp + lp)) + c

    def copy(self, slot, send, dev):
        return pltpu.make_async_remote_copy(
            src_ref=self.buf.at[slot],
            dst_ref=self.buf.at[slot],
            send_sem=send,
            recv_sem=self.rk.at[slot],
            device_id=(self.sec, dev),
            device_id_type=MESH,
        )

    def gather(self, k):
        own = self.slot(self.c, self.ln, self.g)
        return self.copy(own, self.s1.at[k], self.peer(self.ln, (self.g + k) % 4))

    def along(self, gp, n):
        to = self.peer((self.ln + 1 + 2 * n) % 4, self.g)
        return self.copy(self.slot(self.c, self.ln, gp), self.s2.at[2 * gp + n], to)

    def onward(self, gp):
        by = 1 + 2 * (gp // 2)
        source, to = (self.ln + 4 - by) % 4, (self.ln + by) % 4
        return self.copy(self.slot(self.c, source, gp), self.sf.at[gp], self.peer(to, self.g))

    def across(self, lp, gp):
        return self.copy(self.slot(self.c, lp, gp), self.s3.at[4 * lp + gp], self.sibling)

    def arrive(self, t, lp, gp):
        self.copy(self.slot(t, lp, gp), self.s1.at[0], self.sibling).wait_recv()

    def send_own(self):
        @each(4, 1)
        def _(k):
            self.gather(k).start()

        self.pass_on(self.g)

    def pass_on(self, gp):
        @each(2)
        def _(n):
            self.along(gp, n).start()

        self.across(self.ln, gp).start()

    def take_gathered(self):
        @each(4, 1)
        def _(k):
            gp = (self.g + k) % 4
            self.arrive(self.c, self.ln, gp)
            self.pass_on(gp)

    def take_line(self, by):
        lp = (self.ln + by) % 4

        @each(4)
        def _(gp):
            self.arrive(self.c, lp, gp)
            self.across(lp, gp).start()

            @pl.when(by * (1 - gp // 2) + (4 - by) * (gp // 2) == 3)
            def _():
                self.onward(gp).start()

    def take_pair(self, lp):
        @each(4)
        def _(gp):
            self.arrive(1 - self.c, lp, gp)

    def finish(self):
        @each(4, 1)
        def _(k):
            self.gather(k).wait_send()

        @each(4)
        def _(gp):
            self.onward(gp).wait_send()

            @each(2)
            def _(n):
                self.along(gp, n).wait_send()

            @each(4)
            def _(lp):
                self.across(lp, gp).wait_send()


def attn_kernel(gathers, *refs):
    h_ref, gain_ref, qgain_ref, kgain_ref, kvw_ref, w_ref = refs[:6]
    if gathers:
        after_ref, w_out, kv, qs, acc, att, wf, wsem = refs[6:14]
    else:
        after_ref, kv, qs, acc, att, wf, wsem = refs[6:13]
    sems = refs[14:] if gathers else refs[13:]
    me = lax.axis_index("expert")
    sec = lax.axis_index("section")
    y, z, c = me // 8, (me // 2) % 4, me % 2
    g = c * z + (1 - c) * y
    ln = c * y + (1 - c) * z
    tok = h_ref.shape[0]
    kdim = KVH * HEAD
    group = QH // KVH
    rows = group * tok
    span = 4 * tok
    sibling = me + 1 - 2 * c
    kvx = Exchange(kv, *sems[:5], sec, c, g, ln, sibling)

    barrier = pltpu.get_barrier_semaphore()

    def greet(dev):
        pl.semaphore_signal(barrier, inc=1, device_id=(sec, dev), device_id_type=MESH)

    @each(4, 1)
    def _(k):
        greet(kvx.peer(ln, (g + k) % 4))
        greet(kvx.peer((ln + k) % 4, g))

    greet(sibling)
    if gathers:
        wx = Exchange(wf, *sems[5:10], sec, c, g, ln, sibling)
        wf[wx.slot(c, ln, g)] = w_ref[...]
        keep = pltpu.make_async_copy(wf, w_out, wsem)
    else:
        fetch = pltpu.make_async_copy(w_ref, wf, wsem)
        fetch.start()

    r0 = lax.broadcasted_iota(jnp.int32, (256, 256), 0) // HEAD
    c0 = lax.broadcasted_iota(jnp.int32, (256, 256), 1) // HEAD
    averager = jnp.where(r0 == c0, 1.0 / HEAD, 0.0).astype(BF16)

    def head_means(x):
        sq = x * x
        high = sq.astype(BF16)
        low = (sq - high.astype(F32)).astype(BF16)
        return jnp.dot(high, averager, preferred_element_type=F32) + jnp.dot(
            low, averager, preferred_element_type=F32
        )

    h32 = h_ref[...].astype(F32)
    scale = lax.rsqrt(jnp.mean(h32 * h32, axis=-1, keepdims=True) + EPS)
    attn_in = (h32 * scale * gain_ref[...]).astype(BF16)
    kv_raw = jnp.dot(attn_in, kvw_ref[...], preferred_element_type=F32)
    keys = kv_raw[:, :kdim]
    kgain = jnp.concatenate([kgain_ref[...]] * KVH, axis=1)
    keys = keys * lax.rsqrt(head_means(keys) + EPS) * kgain
    kv[kvx.slot(c, ln, g)] = jnp.concatenate([keys, kv_raw[:, kdim:]], axis=1).astype(BF16)

    pl.semaphore_wait(barrier, 7)
    kvx.send_own()

    qgain = jnp.concatenate([qgain_ref[...] * (HEAD**-0.5 * math.log2(math.e))] * 4, axis=1)
    low_half = lax.broadcasted_iota(jnp.int32, (tok, 128), 1) < HEAD
    for t in range(QH * HEAD // 256):
        part = attn_in[:, 256 * t : 256 * t + 256].astype(F32)
        query = part * lax.rsqrt(head_means(part) + EPS) * qgain
        for n in range(4):
            head = 4 * t + n
            at = (head // group) % 2
            tile = query[:, 128 * (n // 2) : 128 * (n // 2) + 128]
            if n % 2 != at:
                tile = pltpu.roll(tile, HEAD, 1)
            tile = jnp.where(low_half == (at == 0), tile, 0.0)
            first = head % group * tok
            qs[head // group, first : first + tok, :] = tile.astype(BF16)
    acc[...] = jnp.zeros_like(acc)

    kvx.take_gathered()
    if gathers:
        wx.send_own()

    ones = jnp.ones((span, 128), BF16)
    qpos = me * tok + lax.broadcasted_iota(jnp.int32, (rows, 1), 0) % tok
    unit = lax.broadcasted_iota(jnp.int32, (1, span), 1)

    def attend_to(t, lp):
        base = t * (8 * lp + 1) + (1 - t) * 2 * lp
        stride = 2 * t + 8 * (1 - t)

        @pl.when(base <= me)
        def _():
            kpos = (base + stride * (unit // tok)) * tok + unit % tok

            @each(KVH)
            def _(head):
                kcols = pl.ds(pl.multiple_of(head // 2 * 128, 128), 128)
                vcols = pl.ds(pl.multiple_of(kdim + head // 2 * 128, 128), 128)
                blocks = pl.ds((t * 4 + lp) * 4, 4)
                keys = kv[blocks, :, kcols].reshape(span, 128)
                values = kv[blocks, :, vcols].reshape(span, 128)
                score = lax.dot_general(
                    qs[head], keys, (((1,), (1,)), ((), ())), preferred_element_type=F32
                )
                expw = jnp.where(kpos <= qpos, jnp.exp2(score), 0.0)
                acc[head] += jnp.dot(
                    expw.astype(BF16),
                    jnp.concatenate([values, ones], axis=1),
                    preferred_element_type=F32,
                )

    @each(4)
    def _(q):
        by = q + q // 2 - 2 * (q // 3)

        @pl.when(q > 0)
        def _():
            kvx.take_line(by)

        attend_to(c, (ln + by) % 4)
        if gathers:

            @pl.when(q == 1)
            def _():
                wx.take_gathered()

            @pl.when(q == 3)
            def _():
                wx.take_line(1)
                wx.take_line(3)

        kvx.take_pair((g + by) % 4)
        attend_to(1 - c, (g + by) % 4)

    def mixed(head, offset):
        at = pl.ds(offset * tok, tok)
        return acc[head, at, :128] / acc[head, at, 128:]

    for lp in range(4):
        for gp in (0, 2):
            first = (2 * lp + gp // 2) * 128
            tile = jnp.where(low_half, mixed(gp, 2 * lp), mixed(gp + 1, 2 * lp))
            att[:, first : first + 128] = tile.astype(BF16)
            one, two = mixed(lp, 2 * gp + 1), mixed(lp, 2 * gp + 3)
            if lp % 2 == 0:
                two = pltpu.roll(two, HEAD, 1)
            else:
                one = pltpu.roll(one, HEAD, 1)
            att[:, 1024 + first : 1024 + first + 128] = jnp.where(low_half, one, two).astype(BF16)

    if gathers:
        wx.take_line(2)

        @each(4)
        def _(lp):
            wx.take_pair(lp)

        keep.start()
    else:
        fetch.wait()

    for n in range(h_ref.shape[1] // 256):
        cols = slice(n * 256, n * 256 + 256)
        made = jnp.dot(
            att[...], wf[:, :, cols].reshape(QH * HEAD, 256), preferred_element_type=F32
        )
        after_ref[:, cols] = h_ref[:, cols].astype(F32) + made

    kvx.finish()
    if gathers:
        wx.finish()
        keep.wait()


def attend(hidden, attn_gain, q_gain, k_gain, kv_w, w, tick):
    tok, d = hidden.shape
    vmem = pl.BlockSpec(memory_space=pltpu.VMEM)
    hbm = pl.BlockSpec(memory_space=pl.ANY)
    dma = pltpu.SemaphoreType.DMA
    gathers = tick == 0
    after = jax.ShapeDtypeStruct((tok, d), F32)
    whole = jax.ShapeDtypeStruct((32, HEAD, d), BF16)
    sems = [dma((4,)), dma((8,)), dma((4,)), dma((16,)), dma((32,))]
    return pl.pallas_call(
        functools.partial(attn_kernel, gathers),
        out_shape=[after, whole] if gathers else [after],
        in_specs=[vmem] * 5 + [vmem if gathers else hbm],
        out_specs=[vmem, hbm] if gathers else [vmem],
        scratch_shapes=[
            pltpu.VMEM((32, tok, 2 * KVH * HEAD), BF16),
            pltpu.VMEM((KVH, QH // KVH * tok, 128), BF16),
            pltpu.VMEM((KVH, QH // KVH * tok, 256), F32),
            pltpu.VMEM((tok, d), BF16),
            pltpu.VMEM((32, HEAD, d), BF16),
            dma,
            *sems,
            *(sems if gathers else []),
        ],
        compiler_params=pltpu.CompilerParams(
            collective_id=2 + tick, has_side_effects=True, vmem_limit_bytes=56 << 20
        ),
        cost_estimate=pl.CostEstimate(
            flops=40 * 10**9, bytes_accessed=20 * 10**6, transcendentals=10**6
        ),
    )(hidden, attn_gain, q_gain, k_gain, kv_w, w)


def moe_kernel(
    cap,
    passes,
    *refs,
):
    if passes:
        after_ref, gain_ref, ids_ref, gates_ref, gu_hbm, dn_hbm, fresh_ref = refs[:7]
        out_ref, next_ref = refs[7:9]
        ob, nb, s5, r5 = refs[-4:]
        refs = refs[9:-4]
    else:
        after_ref, gain_ref, ids_ref, gates_ref, gu_hbm, dn_hbm, out_ref = refs[:7]
        refs = refs[7:]
    (
    xg,
    sb,
    xb,
    bb,
    pb,
    pr,
    pf,
    tot,
    infog,
    sel,
    cw,
    ct,
    gu,
    dn,
    acc,
    hid,
    si,
    ri,
    s1,
    r1,
    s2,
    r2,
    s3,
    r3,
    s4,
    r4,
    wsem,
    ) = refs
    me = lax.axis_index("expert")
    sec = lax.axis_index("section")
    y, z, c = me // 8, (me // 2) % 4, me % 2
    g = c * z + (1 - c) * y
    ln = c * y + (1 - c) * z
    chunks, width = xg.shape[0], xg.shape[3]
    rows = 2 * 4 * cap
    half = 4 * cap
    my_slot = 4 * c + ln
    my_line = 2 * ln + c

    def relay(gp):
        return 2 * (c * (4 * ln + gp) + (1 - c) * (4 * gp + ln)) + c

    def line_dev(i):
        return 2 * (c * (4 * (i // 2) + g) + (1 - c) * (4 * g + i // 2)) + i % 2

    def slot_dev(s):
        t, l0 = s // 4, s % 4
        return (1 - t) * (8 * y + 2 * l0) + t * (8 * l0 + 2 * z + 1)

    def slot_line(s):
        t = s // 4
        return 2 * ((1 - t) * z + t * y) + c

    def remote(src, dst, send, recv, dev):
        return pltpu.make_async_remote_copy(
            src_ref=src,
            dst_ref=dst,
            send_sem=send,
            recv_sem=recv,
            device_id=(sec, dev),
            device_id_type=MESH,
        )

    def info_copy(k):
        gp = (g + k) % 4
        return remote(infog.at[g], infog.at[g], si.at[k], ri.at[g], relay(gp))

    def info_arrival(k):
        gp = (g + k) % 4
        return remote(infog.at[gp], infog.at[gp], si.at[k], ri.at[gp], relay(gp))

    def gather_copy(j, k):
        gp = (g + k) % 4
        return remote(xg.at[j, g], xg.at[j, g], s1.at[j, k], r1.at[j, g], relay(gp))

    def gather_arrival(j, k):
        gp = (g + k) % 4
        return remote(xg.at[j, gp], xg.at[j, gp], s1.at[j, k], r1.at[j, gp], relay(gp))

    def out_copy(j, i):
        return remote(sb.at[j, i], xb.at[j, my_slot], s2.at[j, i], r2.at[j, my_slot], line_dev(i))

    def out_arrival(j, s):
        return remote(xb.at[j, s], xb.at[j, s], s2.at[j, s], r2.at[j, s], slot_dev(s))

    def back_copy(j, s):
        i = slot_line(s)
        return remote(xb.at[j, s], bb.at[j, i], s3.at[j, s], r3.at[j, i], slot_dev(s))

    def back_arrival(j, i):
        return remote(bb.at[j, i], bb.at[j, i], s3.at[j, i], r3.at[j, i], line_dev(i))

    def sum_copy(j, k):
        gp = (g + k) % 4
        return remote(pb.at[j, gp], pr.at[j, g], s4.at[j, k], r4.at[j, g], relay(gp))

    def sum_arrival(j, k):
        gp = (g + k) % 4
        return remote(pr.at[j, gp], pr.at[j, gp], s4.at[j, k], r4.at[j, gp], relay(gp))

    def next_copy(j):
        return pltpu.make_async_remote_copy(
            src_ref=ob.at[j],
            dst_ref=nb.at[j],
            send_sem=s5.at[j],
            recv_sem=r5.at[j],
            device_id=((sec + 1) % 4, me),
            device_id_type=MESH,
        )

    gu_copy = pltpu.make_async_copy(gu_hbm, gu, wsem.at[0])
    dn_copy = pltpu.make_async_copy(dn_hbm, dn, wsem.at[1])

    barrier = pltpu.get_barrier_semaphore()

    def greet(dev):
        pl.semaphore_signal(barrier, inc=1, device_id=(sec, dev), device_id_type=MESH)

    @each(8, 1)
    def _(k):
        greet(8 * y + (2 * z + c + k) % 8)

    @each(4, 1)
    def _(k):
        greet(8 * ((y + k) % 4) + 2 * z)
        greet(8 * ((y + k) % 4) + 2 * z + 1)

    if passes:
        for by in (1, 3):
            pl.semaphore_signal(
                barrier, inc=1, device_id=((sec + by) % 4, me), device_id_type=MESH
            )

    gates = gates_ref[...].astype(F32) * (1.0 / 1024.0)
    infog[g] = route_info(ids_ref[...], gates, 64)
    after = after_ref[...]
    scale = lax.rsqrt(jnp.mean(after * after, axis=-1, keepdims=True) + EPS)
    for j in range(chunks):
        cols = slice(j * width, (j + 1) * width)
        xg[j, g] = (after_ref[:, cols] * scale * gain_ref[:, cols]).astype(BF16)
    pl.semaphore_wait(barrier, 15 if passes else 13)

    @each(4, 1)
    def _(k):
        info_copy(k).start()

    @each(chunks)
    def _(j):
        @each(4, 1)
        def _(k):
            gather_copy(j, k).start()

    gu_copy.start()
    dn_copy.start()
    acc[...] = jnp.zeros_like(acc)

    row = lax.broadcasted_iota(jnp.int32, (half, 512), 0)
    lane = lax.broadcasted_iota(jnp.int32, (half, 512), 1)
    block_of_row = (
        (row >= cap).astype(jnp.int32)
        + (row >= 2 * cap).astype(jnp.int32)
        + (row >= 3 * cap).astype(jnp.int32)
    )
    pattern = jnp.where(block_of_row == lane // 128, row - cap * block_of_row, -5).astype(F32)

    @each(4, 1)
    def _(k):
        info_arrival(k).wait_recv()

    @each(8)
    def _(i):
        dev = line_dev(i)
        picks, gates = [], []
        for e in range(2):
            at = 2 * dev + e
            rank = jnp.concatenate([infog[b, pl.ds(at, 1), :] for b in range(4)], axis=1)
            gate = jnp.concatenate([infog[b, pl.ds(64 + at, 1), :] for b in range(4)], axis=1)
            hit = rank == pattern
            picks.append(jnp.where(hit, 1.0, 0.0))
            gates.append(jnp.where(hit, gate, 0.0))
        at = pl.multiple_of(i * rows, 16)
        sel[pl.ds(at, rows), :] = jnp.concatenate(picks, axis=0).astype(BF16)
        cw[pl.ds(at, rows), :] = jnp.concatenate(gates, axis=0).astype(BF16)

    @each(chunks)
    def _(j):
        @each(4, 1)
        def _(k):
            gather_arrival(j, k).wait_recv()

        @each(width // 256)
        def _(n):
            cols = pl.ds(pl.multiple_of(n * 256, 256), 256)
            held = xg[j, :, :, cols].reshape(512, 256)
            got = jnp.dot(sel[...], held, preferred_element_type=F32)
            sb[j, :, :, cols] = got.astype(BF16).reshape(8, rows, 256)

        @each(8, 1)
        def _(k):
            out_copy(j, (my_line + k) % 8).start()

        xb[j, my_slot] = sb[j, my_line]

    for m in range(8 * rows // 128):
        ct[:, m * 128 : (m + 1) * 128] = (
            cw[m * 128 : (m + 1) * 128, :].astype(F32).T.astype(BF16)
        )

    gu_copy.wait()

    @each(chunks)
    def _(j):
        @each(8, 1)
        def _(k):
            out_arrival(j, (my_slot + k) % 8).wait_recv()

        for e in range(2):
            first = e * (rows - 80)

            @each(acc.shape[2] // 256)
            def _(n):
                cols = pl.ds(pl.multiple_of(n * 256, 256), 256)
                lhs = xb[j, :, first : first + 80, :].reshape(640, width)
                rhs = gu[e, pl.ds(pl.multiple_of(j * width, width), width), cols]
                acc[e, :, cols] += jnp.dot(lhs, rhs, preferred_element_type=F32)

    ff = hid.shape[2]
    for e in range(2):

        @each(640 // 128)
        def _(m):
            at = pl.ds(pl.multiple_of(m * 128, 128), 128)
            hid[e, at, :] = (silu(acc[e, at, :ff]) * acc[e, at, ff:]).astype(BF16)

    dn_copy.wait()

    @each(chunks)
    def _(j):
        @each(width // 256)
        def _(n):
            cols = pl.ds(pl.multiple_of(n * 256, 256), 256)
            at = pl.ds(pl.multiple_of(j * width + n * 256, 256), 256)
            made = [
                jnp.dot(hid[e], dn[e, :, at], preferred_element_type=F32).reshape(8, 80, 256)
                for e in range(2)
            ]
            line = lax.broadcasted_iota(jnp.int32, (8, 16, 256), 1)
            shared = jnp.where(line < 8, made[0][:, 64:80], made[1][:, 0:16])
            xb[j, :, 0:64, cols] = made[0][:, 0:64].astype(BF16)
            xb[j, :, 64:80, cols] = shared.astype(BF16)
            xb[j, :, 80:144, cols] = made[1][:, 16:80].astype(BF16)

        @each(8, 1)
        def _(k):
            back_copy(j, (my_slot + k) % 8).start()

        bb[j, my_line] = xb[j, my_slot]

    @each(chunks)
    def _(j):
        @each(8, 1)
        def _(k):
            back_arrival(j, (my_line + k) % 8).wait_recv()

        @each(width // 256)
        def _(n):
            cols = pl.ds(pl.multiple_of(n * 256, 256), 256)
            at = pl.ds(pl.multiple_of(j * width + n * 256, 256), 256)
            part = jnp.dot(
                ct[...], bb[j, :, :, cols].reshape(8 * rows, 256), preferred_element_type=F32
            ).reshape(4, 128, 256)
            pf[...] = part
            pb[j, :, :, cols] = part.astype(BF16)
            tot[:, at] = after_ref[:, at] + pf[g]

        @each(4, 1)
        def _(k):
            sum_copy(j, k).start()

    @each(chunks)
    def _(j):
        at = pl.ds(pl.multiple_of(j * width, width), width)

        @each(4, 1)
        def _(k):
            sum_arrival(j, k).wait_recv()
            tot[:, at] += pr[j, (g + k) % 4].astype(F32)

        made = tot[:, at].astype(BF16)
        out_ref[:, at] = made
        if passes:
            ob[j] = made
            next_copy(j).start()

    if passes:

        @each(chunks)
        def _(j):
            at = pl.ds(pl.multiple_of(j * width, width), width)
            next_copy(j).wait()
            next_ref[:, at] = jnp.where(sec == 0, fresh_ref[:, at], nb[j])

    @each(4, 1)
    def _(k):
        info_copy(k).wait_send()

    @each(chunks)
    def _(j):
        @each(4, 1)
        def _(k):
            gather_copy(j, k).wait_send()
            sum_copy(j, k).wait_send()

        @each(8, 1)
        def _(k):
            out_copy(j, (my_line + k) % 8).wait_send()
            back_copy(j, (my_slot + k) % 8).wait_send()


def moe_layer(after_attn, gain, ids, gates, gate_up, down, cap, tick, fresh):
    tok, d = after_attn.shape
    ff = down.shape[1]
    w = d // CHUNKS
    rows = 8 * cap
    vmem = pl.BlockSpec(memory_space=pltpu.VMEM)
    hbm = pl.BlockSpec(memory_space=pl.ANY)
    dma = pltpu.SemaphoreType.DMA
    passes = fresh is not None
    outs = 2 if passes else 1
    handed = [
        pltpu.VMEM((CHUNKS, tok, w), BF16),
        pltpu.VMEM((CHUNKS, tok, w), BF16),
        dma((CHUNKS,)),
        dma((CHUNKS,)),
    ]
    return pl.pallas_call(
        functools.partial(moe_kernel, cap, passes),
        out_shape=[jax.ShapeDtypeStruct((tok, d), BF16)] * outs,
        in_specs=[vmem] * 4 + [hbm, hbm] + [vmem] * passes,
        out_specs=[vmem] * outs,
        scratch_shapes=[
            pltpu.VMEM((CHUNKS, 4, tok, w), BF16),
            pltpu.VMEM((CHUNKS, 8, rows, w), BF16),
            pltpu.VMEM((CHUNKS, 8, rows, w), BF16),
            pltpu.VMEM((CHUNKS, 8, rows, w), BF16),
            pltpu.VMEM((CHUNKS, 4, tok, w), BF16),
            pltpu.VMEM((CHUNKS, 4, tok, w), BF16),
            pltpu.VMEM((4, tok, 256), F32),
            pltpu.VMEM((tok, d), F32),
            pltpu.VMEM((4, 128, tok), F32),
            pltpu.VMEM((8 * rows, 4 * tok), BF16),
            pltpu.VMEM((8 * rows, 4 * tok), BF16),
            pltpu.VMEM((4 * tok, 8 * rows), BF16),
            pltpu.VMEM(gate_up.shape, BF16),
            pltpu.VMEM(down.shape, BF16),
            pltpu.VMEM((2, 640, 2 * ff), F32),
            pltpu.VMEM((2, 640, ff), BF16),
            dma((4,)),
            dma((4,)),
            dma((CHUNKS, 4)),
            dma((CHUNKS, 4)),
            dma((CHUNKS, 8)),
            dma((CHUNKS, 8)),
            dma((CHUNKS, 8)),
            dma((CHUNKS, 8)),
            dma((CHUNKS, 4)),
            dma((CHUNKS, 4)),
            dma((2,)),
        ]
        + handed * passes,
        compiler_params=pltpu.CompilerParams(
            collective_id=4 + tick, has_side_effects=True, vmem_limit_bytes=64 << 20
        ),
        cost_estimate=pl.CostEstimate(
            flops=12 * 10**9, bytes_accessed=20 * 10**6, transcendentals=10**6
        ),
    )(after_attn, gain, ids.T, gates.T, gate_up, down, *([fresh] if passes else []))


def body(
    section_input,
    fresh_batch,
    attn_gain,
    query_gain,
    key_gain,
    kv_weight,
    out_weight,
    moe_gain,
    expert_gate_up,
    expert_down,
    route_ids,
    route_weights,
):
    devices = lax.axis_size("expert")
    tok = section_input.shape[1]
    experts_all = expert_gate_up.shape[1] * devices
    cap = tok * TOPK * 9 // (8 * experts_all)

    def layer(hidden, tick, w, fresh):
        after_attn, *w = attend(hidden, attn_gain, query_gain, key_gain, kv_weight[0], w, tick)
        outs = moe_layer(
            after_attn,
            moe_gain,
            route_ids[0, tick],
            route_weights[0, tick],
            expert_gate_up[0],
            expert_down[0],
            cap,
            tick,
            fresh,
        )
        return outs, w

    (first_out, second_in), (out_full,) = layer(section_input[0], 0, out_weight[0], fresh_batch)
    (second_out,), _ = layer(second_in, 1, out_full, None)
    return (first_out[None], second_out[None])


def solution(mesh):
    in_specs = (
        P("section", "expert", None),
        P("expert", None),
        P("section", None),
        P("section", None),
        P("section", None),
        P("section", None, None),
        P("section", "expert", None),
        P("section", None),
        P("section", "expert", None, None),
        P("section", "expert", None, None),
        P("section", None, "expert", None),
        P("section", None, "expert", None),
    )
    out_specs = (P("section", "expert", None), P("section", "expert", None))
    return jax.shard_map(body, mesh=mesh, in_specs=in_specs, out_specs=out_specs, check_vma=False)
```

```python
import functools
import math

import jax
import jax.numpy as jnp
from jax import lax
from jax.experimental import pallas as pl
from jax.experimental.pallas import tpu as pltpu
from jax.sharding import PartitionSpec as P

HEAD = 64
QH = 32
KVH = 4
TOPK = 8
EPS = 1e-06
MESH = pl.DeviceIdType.MESH
CHUNKS = 4
BF16 = jnp.bfloat16
F32 = jnp.float32


def each(n, first=0):
    def wrap(f):
        def step(i, carry):
            f(i)
            return carry

        lax.fori_loop(first, n, step, 0)

    return wrap


def route_info(ids, gates, experts_all):
    topk, tok = ids.shape
    expert = lax.broadcasted_iota(jnp.int32, (experts_all, tok), 0)
    member = jnp.zeros((experts_all, tok), F32)
    weight = jnp.zeros((experts_all, tok), F32)
    for k in range(topk):
        chosen = ids[k : k + 1] == expert
        member += jnp.where(chosen, 1.0, 0.0)
        weight += jnp.where(chosen, gates[k : k + 1], 0.0)
    earlier = lax.broadcasted_iota(jnp.int32, (tok, tok), 0)
    later = lax.broadcasted_iota(jnp.int32, (tok, tok), 1)
    before = jnp.where(earlier < later, 1.0, 0.0).astype(BF16)
    rank = jnp.dot(member.astype(BF16), before, preferred_element_type=F32)
    return jnp.concatenate([jnp.where(member > 0.5, rank, -1.0), weight], axis=0)


def silu(x):
    half = 0.5 * x
    return half + half * jnp.tanh(half)


class Exchange:
    def __init__(self, buf, s1, s2, sf, s3, rk, sec, c, g, ln, sibling):
        self.buf, self.s1, self.s2, self.sf, self.s3, self.rk = buf, s1, s2, sf, s3, rk
        self.sec, self.c, self.g, self.ln, self.sibling = sec, c, g, ln, sibling

    def slot(self, t, lp, gp):
        return (t * 4 + lp) * 4 + gp

    def peer(self, lp, gp):
        c = self.c
        return 2 * (c * (4 * lp + gp) + (1 - c) * (4 * gp + lp)) + c

    def copy(self, slot, send, dev):
        return pltpu.make_async_remote_copy(
            src_ref=self.buf.at[slot],
            dst_ref=self.buf.at[slot],
            send_sem=send,
            recv_sem=self.rk.at[slot],
            device_id=(self.sec, dev),
            device_id_type=MESH,
        )

    def gather(self, k):
        own = self.slot(self.c, self.ln, self.g)
        return self.copy(own, self.s1.at[k], self.peer(self.ln, (self.g + k) % 4))

    def along(self, gp, n):
        to = self.peer((self.ln + 1 + 2 * n) % 4, self.g)
        return self.copy(self.slot(self.c, self.ln, gp), self.s2.at[2 * gp + n], to)

    def onward(self, gp):
        by = 1 + 2 * (gp // 2)
        source, to = (self.ln + 4 - by) % 4, (self.ln + by) % 4
        return self.copy(self.slot(self.c, source, gp), self.sf.at[gp], self.peer(to, self.g))

    def across(self, lp, gp):
        return self.copy(self.slot(self.c, lp, gp), self.s3.at[4 * lp + gp], self.sibling)

    def arrive(self, t, lp, gp):
        self.copy(self.slot(t, lp, gp), self.s1.at[0], self.sibling).wait_recv()

    def send_own(self):
        @each(4, 1)
        def _(k):
            self.gather(k).start()

        self.pass_on(self.g)

    def pass_on(self, gp):
        @each(2)
        def _(n):
            self.along(gp, n).start()

        self.across(self.ln, gp).start()

    def take_gathered(self):
        @each(4, 1)
        def _(k):
            gp = (self.g + k) % 4
            self.arrive(self.c, self.ln, gp)
            self.pass_on(gp)

    def take_line(self, by):
        lp = (self.ln + by) % 4

        @each(4)
        def _(gp):
            self.arrive(self.c, lp, gp)
            self.across(lp, gp).start()

            @pl.when(by * (1 - gp // 2) + (4 - by) * (gp // 2) == 3)
            def _():
                self.onward(gp).start()

    def take_pair(self, lp):
        @each(4)
        def _(gp):
            self.arrive(1 - self.c, lp, gp)

    def finish(self):
        @each(4, 1)
        def _(k):
            self.gather(k).wait_send()

        @each(4)
        def _(gp):
            self.onward(gp).wait_send()

            @each(2)
            def _(n):
                self.along(gp, n).wait_send()

            @each(4)
            def _(lp):
                self.across(lp, gp).wait_send()


def attn_kernel(gathers, *refs):
    h_ref, gain_ref, qgain_ref, kgain_ref, kvw_ref, w_ref = refs[:6]
    if gathers:
        after_ref, w_out, kv, qs, acc, att, wf, wsem = refs[6:14]
    else:
        after_ref, kv, qs, acc, att, wf, wsem = refs[6:13]
    sems = refs[14:] if gathers else refs[13:]
    me = lax.axis_index("expert")
    sec = lax.axis_index("section")
    y, z, c = me // 8, (me // 2) % 4, me % 2
    g = c * z + (1 - c) * y
    ln = c * y + (1 - c) * z
    tok = h_ref.shape[0]
    kdim = KVH * HEAD
    group = QH // KVH
    rows = group * tok
    span = 4 * tok
    sibling = me + 1 - 2 * c
    kvx = Exchange(kv, *sems[:5], sec, c, g, ln, sibling)

    barrier = pltpu.get_barrier_semaphore()

    def greet(dev):
        pl.semaphore_signal(barrier, inc=1, device_id=(sec, dev), device_id_type=MESH)

    @each(4, 1)
    def _(k):
        greet(kvx.peer(ln, (g + k) % 4))
        greet(kvx.peer((ln + k) % 4, g))

    greet(sibling)
    if gathers:
        wx = Exchange(wf, *sems[5:10], sec, c, g, ln, sibling)
        wf[wx.slot(c, ln, g)] = w_ref[...]
        keep = pltpu.make_async_copy(wf, w_out, wsem)
    else:
        fetch = pltpu.make_async_copy(w_ref, wf, wsem)
        fetch.start()

    pl.semaphore_wait(barrier, 7)
    if gathers:
        wx.send_own()

    r0 = lax.broadcasted_iota(jnp.int32, (256, 256), 0) // HEAD
    c0 = lax.broadcasted_iota(jnp.int32, (256, 256), 1) // HEAD
    averager = jnp.where(r0 == c0, 1.0 / HEAD, 0.0).astype(BF16)

    def head_means(x):
        sq = x * x
        high = sq.astype(BF16)
        low = (sq - high.astype(F32)).astype(BF16)
        return jnp.dot(high, averager, preferred_element_type=F32) + jnp.dot(
            low, averager, preferred_element_type=F32
        )

    h32 = h_ref[...].astype(F32)
    scale = lax.rsqrt(jnp.mean(h32 * h32, axis=-1, keepdims=True) + EPS)
    attn_in = (h32 * scale * gain_ref[...]).astype(BF16)
    kv_raw = jnp.dot(attn_in, kvw_ref[...], preferred_element_type=F32)
    keys = kv_raw[:, :kdim]
    kgain = jnp.concatenate([kgain_ref[...]] * KVH, axis=1)
    keys = keys * lax.rsqrt(head_means(keys) + EPS) * kgain
    kv[kvx.slot(c, ln, g)] = jnp.concatenate([keys, kv_raw[:, kdim:]], axis=1).astype(BF16)

    kvx.send_own()

    qgain = jnp.concatenate([qgain_ref[...] * (HEAD**-0.5 * math.log2(math.e))] * 4, axis=1)
    low_half = lax.broadcasted_iota(jnp.int32, (tok, 128), 1) < HEAD
    for t in range(QH * HEAD // 256):
        part = attn_in[:, 256 * t : 256 * t + 256].astype(F32)
        query = part * lax.rsqrt(head_means(part) + EPS) * qgain
        for n in range(4):
            head = 4 * t + n
            at = (head // group) % 2
            tile = query[:, 128 * (n // 2) : 128 * (n // 2) + 128]
            if n % 2 != at:
                tile = pltpu.roll(tile, HEAD, 1)
            tile = jnp.where(low_half == (at == 0), tile, 0.0)
            first = head % group * tok
            qs[head // group, first : first + tok, :] = tile.astype(BF16)
    acc[...] = jnp.zeros_like(acc)

    kvx.take_gathered()
    if gathers:
        wx.take_gathered()

    qpos = me * tok + lax.broadcasted_iota(jnp.int32, (rows, 1), 0) % tok
    unit = lax.broadcasted_iota(jnp.int32, (1, span), 1)

    def attend_to(t, lp):
        base = t * (8 * lp + 1) + (1 - t) * 2 * lp
        stride = 2 * t + 8 * (1 - t)

        @pl.when(base <= me)
        def _():
            kpos = (base + stride * (unit // tok)) * tok + unit % tok

            @each(KVH)
            def _(head):
                kcols = pl.ds(pl.multiple_of(head // 2 * 128, 128), 128)
                vcols = pl.ds(pl.multiple_of(kdim + head // 2 * 128, 128), 128)
                blocks = pl.ds((t * 4 + lp) * 4, 4)
                keys = kv[blocks, :, kcols].reshape(span, 128)
                values = kv[blocks, :, vcols].reshape(span, 128)
                own = (lax.broadcasted_iota(jnp.int32, (span, 128), 1) // HEAD) == head % 2
                value = jnp.where(own, values.astype(F32), 1.0).astype(BF16)
                score = lax.dot_general(
                    qs[head], keys, (((1,), (1,)), ((), ())), preferred_element_type=F32
                )
                expw = jnp.where(kpos <= qpos, jnp.exp2(score), 0.0)
                acc[head] += jnp.dot(
                    expw.astype(BF16),
                    value,
                    preferred_element_type=F32,
                )

    @each(4)
    def _(q):
        by = q + q // 2 - 2 * (q // 3)

        if gathers:

            @pl.when(q == 3)
            def _():
                wx.take_line(1)
                wx.take_line(3)

        @pl.when(q > 0)
        def _():
            kvx.take_line(by)

        attend_to(c, (ln + by) % 4)
        kvx.take_pair((g + by) % 4)
        attend_to(1 - c, (g + by) % 4)

    def mixed(head, offset):
        at = pl.ds(offset * tok, tok)
        both = acc[head, at, :]
        return both / pltpu.roll(both, HEAD, 1)

    for lp in range(4):
        for gp in (0, 2):
            cols = slice((4 * lp + gp) * HEAD, (4 * lp + gp) * HEAD + 128)
            far = slice(1024 + cols.start, 1024 + cols.stop)
            tile = jnp.where(low_half, mixed(gp, 2 * lp), mixed(gp + 1, 2 * lp))
            att[:, cols] = tile.astype(BF16)
            one, two = mixed(lp, 2 * gp + 1), mixed(lp, 2 * gp + 3)
            if lp % 2 == 0:
                two = pltpu.roll(two, HEAD, 1)
            else:
                one = pltpu.roll(one, HEAD, 1)
            att[:, far] = jnp.where(low_half, one, two).astype(BF16)

    if gathers:
        wx.take_line(2)

        @each(4)
        def _(lp):
            wx.take_pair(lp)

        keep.start()
    else:
        fetch.wait()

    for n in range(h_ref.shape[1] // 256):
        cols = slice(n * 256, n * 256 + 256)
        made = jnp.dot(
            att[...], wf[:, :, cols].reshape(QH * HEAD, 256), preferred_element_type=F32
        )
        after_ref[:, cols] = h_ref[:, cols].astype(F32) + made

    kvx.finish()
    if gathers:
        wx.finish()
        keep.wait()


def attend(hidden, attn_gain, q_gain, k_gain, kv_w, w, tick):
    tok, d = hidden.shape
    vmem = pl.BlockSpec(memory_space=pltpu.VMEM)
    hbm = pl.BlockSpec(memory_space=pl.ANY)
    dma = pltpu.SemaphoreType.DMA
    gathers = tick == 0
    after = jax.ShapeDtypeStruct((tok, d), F32)
    whole = jax.ShapeDtypeStruct((32, HEAD, d), BF16)
    sems = [dma((4,)), dma((8,)), dma((4,)), dma((16,)), dma((32,))]
    return pl.pallas_call(
        functools.partial(attn_kernel, gathers),
        out_shape=[after, whole] if gathers else [after],
        in_specs=[vmem] * 5 + [vmem if gathers else hbm],
        out_specs=[vmem, hbm] if gathers else [vmem],
        scratch_shapes=[
            pltpu.VMEM((32, tok, 2 * KVH * HEAD), BF16),
            pltpu.VMEM((KVH, QH // KVH * tok, 128), BF16),
            pltpu.VMEM((KVH, QH // KVH * tok, 128), F32),
            pltpu.VMEM((tok, d), BF16),
            pltpu.VMEM((32, HEAD, d), BF16),
            dma,
            *sems,
            *(sems if gathers else []),
        ],
        compiler_params=pltpu.CompilerParams(
            collective_id=2 + tick, has_side_effects=True, vmem_limit_bytes=56 << 20
        ),
        cost_estimate=pl.CostEstimate(
            flops=40 * 10**9, bytes_accessed=20 * 10**6, transcendentals=10**6
        ),
    )(hidden, attn_gain, q_gain, k_gain, kv_w, w)


def moe_kernel(
    cap,
    tick,
    passes,
    *refs,
):
    if passes:
        after_ref, gain_ref, ids_ref, gates_ref, gu_hbm, dn_hbm, fresh_ref = refs[:7]
        out_ref, next_ref = refs[7:9]
        ob, nb, s5, r5 = refs[-4:]
        refs = refs[9:-4]
    else:
        after_ref, gain_ref, ids_ref, gates_ref, gu_hbm, dn_hbm, out_ref = refs[:7]
        refs = refs[7:]
    (
    xg,
    sb,
    xb,
    bb,
    pb,
    pr,
    pf,
    tot,
    infog,
    sel,
    cw,
    ct,
    gu,
    dn,
    acc,
    hid,
    si,
    ri,
    s1,
    r1,
    s2,
    r2,
    s3,
    r3,
    s4,
    r4,
    wsem,
    ) = refs
    me = lax.axis_index("expert")
    sec = lax.axis_index("section")
    y, z, c = me // 8, (me // 2) % 4, me % 2
    g = c * z + (1 - c) * y
    ln = c * y + (1 - c) * z
    chunks, width = xg.shape[0], xg.shape[3]
    rows = 2 * 4 * cap
    half = 4 * cap
    my_slot = 4 * c + ln
    my_line = 2 * ln + c

    def relay(gp):
        return 2 * (c * (4 * ln + gp) + (1 - c) * (4 * gp + ln)) + c

    def line_dev(i):
        return 2 * (c * (4 * (i // 2) + g) + (1 - c) * (4 * g + i // 2)) + i % 2

    def slot_dev(s):
        t, l0 = s // 4, s % 4
        return (1 - t) * (8 * y + 2 * l0) + t * (8 * l0 + 2 * z + 1)

    def slot_line(s):
        t = s // 4
        return 2 * ((1 - t) * z + t * y) + c

    def remote(src, dst, send, recv, dev):
        return pltpu.make_async_remote_copy(
            src_ref=src,
            dst_ref=dst,
            send_sem=send,
            recv_sem=recv,
            device_id=(sec, dev),
            device_id_type=MESH,
        )

    def info_copy(k):
        gp = (g + k) % 4
        return remote(infog.at[g], infog.at[g], si.at[k], ri.at[g], relay(gp))

    def info_arrival(k):
        gp = (g + k) % 4
        return remote(infog.at[gp], infog.at[gp], si.at[k], ri.at[gp], relay(gp))

    def gather_copy(j, k):
        gp = (g + k) % 4
        return remote(xg.at[j, g], xg.at[j, g], s1.at[j, k], r1.at[j, g], relay(gp))

    def gather_arrival(j, k):
        gp = (g + k) % 4
        return remote(xg.at[j, gp], xg.at[j, gp], s1.at[j, k], r1.at[j, gp], relay(gp))

    def out_copy(j, i):
        return remote(sb.at[j, i], xb.at[j, my_slot], s2.at[j, i], r2.at[j, my_slot], line_dev(i))

    def out_arrival(j, s):
        return remote(xb.at[j, s], xb.at[j, s], s2.at[j, s], r2.at[j, s], slot_dev(s))

    def back_copy(j, s):
        i = slot_line(s)
        return remote(xb.at[j, s], bb.at[j, i], s3.at[j, s], r3.at[j, i], slot_dev(s))

    def back_arrival(j, i):
        return remote(bb.at[j, i], bb.at[j, i], s3.at[j, i], r3.at[j, i], line_dev(i))

    def sum_copy(j, k):
        gp = (g + k) % 4
        return remote(pb.at[j, gp], pr.at[j, g], s4.at[j, k], r4.at[j, g], relay(gp))

    def sum_arrival(j, k):
        gp = (g + k) % 4
        return remote(pr.at[j, gp], pr.at[j, gp], s4.at[j, k], r4.at[j, gp], relay(gp))

    def next_copy(j):
        return pltpu.make_async_remote_copy(
            src_ref=ob.at[j],
            dst_ref=nb.at[j],
            send_sem=s5.at[j],
            recv_sem=r5.at[j],
            device_id=((sec + 1) % 4, me),
            device_id_type=MESH,
        )

    gu_copy = pltpu.make_async_copy(gu_hbm, gu, wsem.at[0])
    dn_copy = pltpu.make_async_copy(dn_hbm, dn, wsem.at[1])

    barrier = pltpu.get_barrier_semaphore()

    def greet(dev):
        pl.semaphore_signal(barrier, inc=1, device_id=(sec, dev), device_id_type=MESH)

    @each(8, 1)
    def _(k):
        greet(8 * y + (2 * z + c + k) % 8)

    @each(4, 1)
    def _(k):
        greet(8 * ((y + k) % 4) + 2 * z)
        greet(8 * ((y + k) % 4) + 2 * z + 1)

    if passes:
        for by in (1, 3):
            pl.semaphore_signal(
                barrier, inc=1, device_id=((sec + by) % 4, me), device_id_type=MESH
            )

    gates = gates_ref[tick].astype(F32) * (1.0 / 1024.0)
    infog[g] = route_info(ids_ref[tick], gates, 64)
    after = after_ref[...]
    scale = lax.rsqrt(jnp.mean(after * after, axis=-1, keepdims=True) + EPS)
    for j in range(chunks):
        cols = slice(j * width, (j + 1) * width)
        xg[j, g] = (after_ref[:, cols] * scale * gain_ref[:, cols]).astype(BF16)
    pl.semaphore_wait(barrier, 15 if passes else 13)

    @each(4, 1)
    def _(k):
        info_copy(k).start()

    @each(chunks)
    def _(j):
        @each(4, 1)
        def _(k):
            gather_copy(j, k).start()

    gu_copy.start()
    dn_copy.start()
    row = lax.broadcasted_iota(jnp.int32, (half, 512), 0)
    lane = lax.broadcasted_iota(jnp.int32, (half, 512), 1)
    block_of_row = (
        (row >= cap).astype(jnp.int32)
        + (row >= 2 * cap).astype(jnp.int32)
        + (row >= 3 * cap).astype(jnp.int32)
    )
    pattern = jnp.where(block_of_row == lane // 128, row - cap * block_of_row, -5).astype(F32)

    @each(4, 1)
    def _(k):
        info_arrival(k).wait_recv()

    def hits(i, e):
        at = 2 * line_dev(i) + e
        rank = jnp.concatenate([infog[b, pl.ds(at, 1), :] for b in range(4)], axis=1)
        return rank == pattern

    @each(8)
    def _(i):
        picks = [jnp.where(hits(i, e), 1.0, 0.0) for e in range(2)]
        at = pl.multiple_of(i * rows, 16)
        sel[pl.ds(at, rows), :] = jnp.concatenate(picks, axis=0).astype(BF16)

    @each(chunks)
    def _(j):
        @each(4, 1)
        def _(k):
            gather_arrival(j, k).wait_recv()

        @each(width // 256)
        def _(n):
            cols = pl.ds(pl.multiple_of(n * 256, 256), 256)
            held = xg[j, :, :, cols].reshape(512, 256)
            got = jnp.dot(sel[...], held, preferred_element_type=F32)
            sb[j, :, :, cols] = got.astype(BF16).reshape(8, rows, 256)

        @each(8, 1)
        def _(k):
            out_copy(j, (my_line + k) % 8).start()

        xb[j, my_slot] = sb[j, my_line]

    @each(8)
    def _(i):
        gates = []
        for e in range(2):
            at = 64 + 2 * line_dev(i) + e
            gate = jnp.concatenate([infog[b, pl.ds(at, 1), :] for b in range(4)], axis=1)
            gates.append(jnp.where(hits(i, e), gate, 0.0))
        at = pl.multiple_of(i * rows, 16)
        cw[pl.ds(at, rows), :] = jnp.concatenate(gates, axis=0).astype(BF16)

    for m in range(8 * rows // 128):
        ct[:, m * 128 : (m + 1) * 128] = (
            cw[m * 128 : (m + 1) * 128, :].astype(F32).T.astype(BF16)
        )

    acc[...] = jnp.zeros_like(acc)
    gu_copy.wait()

    @each(chunks)
    def _(j):
        @each(8, 1)
        def _(k):
            out_arrival(j, (my_slot + k) % 8).wait_recv()

        for e in range(2):
            first = e * (rows - 80)

            @each(acc.shape[2] // 256)
            def _(n):
                cols = pl.ds(pl.multiple_of(n * 256, 256), 256)
                lhs = xb[j, :, first : first + 80, :].reshape(640, width)
                rhs = gu[e, pl.ds(pl.multiple_of(j * width, width), width), cols]
                acc[e, :, cols] += jnp.dot(lhs, rhs, preferred_element_type=F32)

    ff = hid.shape[2]
    for e in range(2):

        @each(640 // 128)
        def _(m):
            at = pl.ds(pl.multiple_of(m * 128, 128), 128)
            hid[e, at, :] = (silu(acc[e, at, :ff]) * acc[e, at, ff:]).astype(BF16)

    dn_copy.wait()

    @each(chunks)
    def _(j):
        @each(width // 256)
        def _(n):
            cols = pl.ds(pl.multiple_of(n * 256, 256), 256)
            at = pl.ds(pl.multiple_of(j * width + n * 256, 256), 256)
            made = [
                jnp.dot(hid[e], dn[e, :, at], preferred_element_type=F32).reshape(8, 80, 256)
                for e in range(2)
            ]
            line = lax.broadcasted_iota(jnp.int32, (8, 16, 256), 1)
            shared = jnp.where(line < 8, made[0][:, 64:80], made[1][:, 0:16])
            xb[j, :, 0:64, cols] = made[0][:, 0:64].astype(BF16)
            xb[j, :, 64:80, cols] = shared.astype(BF16)
            xb[j, :, 80:144, cols] = made[1][:, 16:80].astype(BF16)

        @each(8, 1)
        def _(k):
            back_copy(j, (my_slot + k) % 8).start()

        bb[j, my_line] = xb[j, my_slot]

    @each(chunks)
    def _(j):
        @each(8, 1)
        def _(k):
            back_arrival(j, (my_line + k) % 8).wait_recv()

        @each(width // 256)
        def _(n):
            cols = pl.ds(pl.multiple_of(n * 256, 256), 256)
            at = pl.ds(pl.multiple_of(j * width + n * 256, 256), 256)
            part = jnp.dot(
                ct[...], bb[j, :, :, cols].reshape(8 * rows, 256), preferred_element_type=F32
            ).reshape(4, 128, 256)
            pf[...] = part
            pb[j, :, :, cols] = part.astype(BF16)
            tot[:, at] = after_ref[:, at] + pf[g]

        @each(4, 1)
        def _(k):
            sum_copy(j, k).start()

    @each(chunks)
    def _(j):
        at = pl.ds(pl.multiple_of(j * width, width), width)

        @each(4, 1)
        def _(k):
            sum_arrival(j, k).wait_recv()
            tot[:, at] += pr[j, (g + k) % 4].astype(F32)

        made = tot[:, at].astype(BF16)
        out_ref[:, at] = made
        if passes:
            ob[j] = made
            next_copy(j).start()

    if passes:

        @each(chunks)
        def _(j):
            at = pl.ds(pl.multiple_of(j * width, width), width)
            next_copy(j).wait()
            next_ref[:, at] = jnp.where(sec == 0, fresh_ref[:, at], nb[j])

    @each(4, 1)
    def _(k):
        info_copy(k).wait_send()

    @each(chunks)
    def _(j):
        @each(4, 1)
        def _(k):
            gather_copy(j, k).wait_send()
            sum_copy(j, k).wait_send()

        @each(8, 1)
        def _(k):
            out_copy(j, (my_line + k) % 8).wait_send()
            back_copy(j, (my_slot + k) % 8).wait_send()


def moe_layer(after_attn, gain, ids, gates, gate_up, down, cap, tick, fresh):
    tok, d = after_attn.shape
    ff = down.shape[1]
    w = d // CHUNKS
    rows = 8 * cap
    vmem = pl.BlockSpec(memory_space=pltpu.VMEM)
    hbm = pl.BlockSpec(memory_space=pl.ANY)
    dma = pltpu.SemaphoreType.DMA
    passes = fresh is not None
    outs = 2 if passes else 1
    handed = [
        pltpu.VMEM((CHUNKS, tok, w), BF16),
        pltpu.VMEM((CHUNKS, tok, w), BF16),
        dma((CHUNKS,)),
        dma((CHUNKS,)),
    ]
    return pl.pallas_call(
        functools.partial(moe_kernel, cap, tick, passes),
        out_shape=[jax.ShapeDtypeStruct((tok, d), BF16)] * outs,
        in_specs=[vmem] * 4 + [hbm, hbm] + [vmem] * passes,
        out_specs=[vmem] * outs,
        scratch_shapes=[
            pltpu.VMEM((CHUNKS, 4, tok, w), BF16),
            pltpu.VMEM((CHUNKS, 8, rows, w), BF16),
            pltpu.VMEM((CHUNKS, 8, rows, w), BF16),
            pltpu.VMEM((CHUNKS, 8, rows, w), BF16),
            pltpu.VMEM((CHUNKS, 4, tok, w), BF16),
            pltpu.VMEM((CHUNKS, 4, tok, w), BF16),
            pltpu.VMEM((4, tok, 256), F32),
            pltpu.VMEM((tok, d), F32),
            pltpu.VMEM((4, 128, tok), F32),
            pltpu.VMEM((8 * rows, 4 * tok), BF16),
            pltpu.VMEM((8 * rows, 4 * tok), BF16),
            pltpu.VMEM((4 * tok, 8 * rows), BF16),
            pltpu.VMEM(gate_up.shape, BF16),
            pltpu.VMEM(down.shape, BF16),
            pltpu.VMEM((2, 640, 2 * ff), F32),
            pltpu.VMEM((2, 640, ff), BF16),
            dma((4,)),
            dma((4,)),
            dma((CHUNKS, 4)),
            dma((CHUNKS, 4)),
            dma((CHUNKS, 8)),
            dma((CHUNKS, 8)),
            dma((CHUNKS, 8)),
            dma((CHUNKS, 8)),
            dma((CHUNKS, 4)),
            dma((CHUNKS, 4)),
            dma((2,)),
        ]
        + handed * passes,
        compiler_params=pltpu.CompilerParams(
            collective_id=4 + tick, has_side_effects=True, vmem_limit_bytes=64 << 20
        ),
        cost_estimate=pl.CostEstimate(
            flops=12 * 10**9, bytes_accessed=20 * 10**6, transcendentals=10**6
        ),
    )(after_attn, gain, ids, gates, gate_up, down, *([fresh] if passes else []))


def body(
    section_input,
    fresh_batch,
    attn_gain,
    query_gain,
    key_gain,
    kv_weight,
    out_weight,
    moe_gain,
    expert_gate_up,
    expert_down,
    route_ids,
    route_weights,
):
    devices = lax.axis_size("expert")
    tok = section_input.shape[1]
    experts_all = expert_gate_up.shape[1] * devices
    cap = tok * TOPK * 9 // (8 * experts_all)

    def layer(hidden, tick, w, fresh):
        after_attn, *w = attend(hidden, attn_gain, query_gain, key_gain, kv_weight[0], w, tick)
        outs = moe_layer(
            after_attn,
            moe_gain,
            route_ids[0].transpose(0, 2, 1),
            route_weights[0].transpose(0, 2, 1),
            expert_gate_up[0],
            expert_down[0],
            cap,
            tick,
            fresh,
        )
        return outs, w

    (first_out, second_in), (out_full,) = layer(section_input[0], 0, out_weight[0], fresh_batch)
    (second_out,), _ = layer(second_in, 1, out_full, None)
    return (first_out[None], second_out[None])


def solution(mesh):
    in_specs = (
        P("section", "expert", None),
        P("expert", None),
        P("section", None),
        P("section", None),
        P("section", None),
        P("section", None, None),
        P("section", "expert", None),
        P("section", None),
        P("section", "expert", None, None),
        P("section", "expert", None, None),
        P("section", None, "expert", None),
        P("section", None, "expert", None),
    )
    out_specs = (P("section", "expert", None), P("section", "expert", None))
    return jax.shard_map(body, mesh=mesh, in_specs=in_specs, out_specs=out_specs, check_vma=False)
```

```python
import functools
import math

import jax
import jax.numpy as jnp
from jax import lax
from jax.experimental import pallas as pl
from jax.experimental.pallas import tpu as pltpu
from jax.sharding import PartitionSpec as P

HEAD = 64
QH = 32
KVH = 4
TOPK = 8
EPS = 1e-06
MESH = pl.DeviceIdType.MESH
CHUNKS = 4
BF16 = jnp.bfloat16
F32 = jnp.float32


def each(n, first=0):
    def wrap(f):
        def step(i, carry):
            f(i)
            return carry

        lax.fori_loop(first, n, step, 0)

    return wrap


def route_info(ids, gates, experts_all):
    topk, tok = ids.shape
    expert = lax.broadcasted_iota(jnp.int32, (experts_all, tok), 0)
    member = jnp.zeros((experts_all, tok), F32)
    weight = jnp.zeros((experts_all, tok), F32)
    for k in range(topk):
        chosen = ids[k : k + 1] == expert
        member += jnp.where(chosen, 1.0, 0.0)
        weight += jnp.where(chosen, gates[k : k + 1], 0.0)
    earlier = lax.broadcasted_iota(jnp.int32, (tok, tok), 0)
    later = lax.broadcasted_iota(jnp.int32, (tok, tok), 1)
    before = jnp.where(earlier < later, 1.0, 0.0).astype(BF16)
    rank = jnp.dot(member.astype(BF16), before, preferred_element_type=F32)
    return jnp.concatenate([jnp.where(member > 0.5, rank, -1.0), weight], axis=0)


def silu(x):
    half = 0.5 * x
    return half + half * jnp.tanh(half)


class Exchange:
    def __init__(self, buf, s1, s2, sf, s3, rk, sec, c, g, ln, sibling):
        self.buf, self.s1, self.s2, self.sf, self.s3, self.rk = buf, s1, s2, sf, s3, rk
        self.sec, self.c, self.g, self.ln, self.sibling = sec, c, g, ln, sibling

    def slot(self, t, lp, gp):
        return (t * 4 + lp) * 4 + gp

    def peer(self, lp, gp):
        c = self.c
        return 2 * (c * (4 * lp + gp) + (1 - c) * (4 * gp + lp)) + c

    def copy(self, slot, send, dev):
        return pltpu.make_async_remote_copy(
            src_ref=self.buf.at[slot],
            dst_ref=self.buf.at[slot],
            send_sem=send,
            recv_sem=self.rk.at[slot],
            device_id=(self.sec, dev),
            device_id_type=MESH,
        )

    def gather(self, k):
        own = self.slot(self.c, self.ln, self.g)
        return self.copy(own, self.s1.at[k], self.peer(self.ln, (self.g + k) % 4))

    def along(self, gp, n):
        to = self.peer((self.ln + 1 + 2 * n) % 4, self.g)
        return self.copy(self.slot(self.c, self.ln, gp), self.s2.at[2 * gp + n], to)

    def onward(self, gp):
        by = 1 + 2 * (gp // 2)
        source, to = (self.ln + 4 - by) % 4, (self.ln + by) % 4
        return self.copy(self.slot(self.c, source, gp), self.sf.at[gp], self.peer(to, self.g))

    def across(self, lp, gp):
        return self.copy(self.slot(self.c, lp, gp), self.s3.at[4 * lp + gp], self.sibling)

    def arrive(self, t, lp, gp):
        self.copy(self.slot(t, lp, gp), self.s1.at[0], self.sibling).wait_recv()

    def send_own(self):
        @each(4, 1)
        def _(k):
            self.gather(k).start()

        self.pass_on(self.g)

    def pass_on(self, gp):
        @each(2)
        def _(n):
            self.along(gp, n).start()

        self.across(self.ln, gp).start()

    def take_gathered(self):
        @each(4, 1)
        def _(k):
            gp = (self.g + k) % 4
            self.arrive(self.c, self.ln, gp)
            self.pass_on(gp)

    def take_line(self, by):
        lp = (self.ln + by) % 4

        @each(4)
        def _(gp):
            self.arrive(self.c, lp, gp)
            self.across(lp, gp).start()

            @pl.when(by * (1 - gp // 2) + (4 - by) * (gp // 2) == 3)
            def _():
                self.onward(gp).start()

    def take_pair(self, lp):
        @each(4)
        def _(gp):
            self.arrive(1 - self.c, lp, gp)

    def finish(self):
        @each(4, 1)
        def _(k):
            self.gather(k).wait_send()

        @each(4)
        def _(gp):
            self.onward(gp).wait_send()

            @each(2)
            def _(n):
                self.along(gp, n).wait_send()

            @each(4)
            def _(lp):
                self.across(lp, gp).wait_send()


def attn_kernel(gathers, *refs):
    h_ref, gain_ref, qgain_ref, kgain_ref, kvw_ref, w_ref = refs[:6]
    if gathers:
        after_ref, w_out, kv, qs, acc, att, wf, wsem = refs[6:14]
    else:
        after_ref, kv, qs, acc, att, wf, wsem = refs[6:13]
    sems = refs[14:] if gathers else refs[13:]
    me = lax.axis_index("expert")
    sec = lax.axis_index("section")
    y, z, c = me // 8, (me // 2) % 4, me % 2
    g = c * z + (1 - c) * y
    ln = c * y + (1 - c) * z
    tok = h_ref.shape[0]
    kdim = KVH * HEAD
    group = QH // KVH
    rows = group * tok
    span = 4 * tok
    sibling = me + 1 - 2 * c
    kvx = Exchange(kv, *sems[:5], sec, c, g, ln, sibling)

    barrier = pltpu.get_barrier_semaphore()

    def greet(dev):
        pl.semaphore_signal(barrier, inc=1, device_id=(sec, dev), device_id_type=MESH)

    @each(4, 1)
    def _(k):
        greet(kvx.peer(ln, (g + k) % 4))
        greet(kvx.peer((ln + k) % 4, g))

    greet(sibling)
    if gathers:
        wx = Exchange(wf, *sems[5:10], sec, c, g, ln, sibling)
        wf[wx.slot(c, ln, g)] = w_ref[...]
        keep = pltpu.make_async_copy(wf, w_out, wsem)
    else:
        fetch = pltpu.make_async_copy(w_ref, wf, wsem)
        fetch.start()

    pl.semaphore_wait(barrier, 7)
    if gathers:
        wx.send_own()

    r0 = lax.broadcasted_iota(jnp.int32, (256, 256), 0) // HEAD
    c0 = lax.broadcasted_iota(jnp.int32, (256, 256), 1) // HEAD
    averager = jnp.where(r0 == c0, 1.0 / HEAD, 0.0).astype(BF16)

    def head_means(x):
        sq = x * x
        high = sq.astype(BF16)
        low = (sq - high.astype(F32)).astype(BF16)
        return jnp.dot(high, averager, preferred_element_type=F32) + jnp.dot(
            low, averager, preferred_element_type=F32
        )

    h32 = h_ref[...].astype(F32)
    scale = lax.rsqrt(jnp.mean(h32 * h32, axis=-1, keepdims=True) + EPS)
    attn_in = (h32 * scale * gain_ref[...]).astype(BF16)
    kv_raw = jnp.dot(attn_in, kvw_ref[...], preferred_element_type=F32)
    keys = kv_raw[:, :kdim]
    kgain = jnp.concatenate([kgain_ref[...]] * KVH, axis=1)
    keys = keys * lax.rsqrt(head_means(keys) + EPS) * kgain
    kv[kvx.slot(c, ln, g)] = jnp.concatenate([keys, kv_raw[:, kdim:]], axis=1).astype(BF16)

    kvx.send_own()

    qgain = jnp.concatenate([qgain_ref[...] * (HEAD**-0.5 * math.log2(math.e))] * 4, axis=1)
    low_half = lax.broadcasted_iota(jnp.int32, (tok, 128), 1) < HEAD
    for t in range(QH * HEAD // 256):
        part = attn_in[:, 256 * t : 256 * t + 256].astype(F32)
        query = part * lax.rsqrt(head_means(part) + EPS) * qgain
        for n in range(4):
            head = 4 * t + n
            at = (head // group) % 2
            tile = query[:, 128 * (n // 2) : 128 * (n // 2) + 128]
            if n % 2 != at:
                tile = pltpu.roll(tile, HEAD, 1)
            tile = jnp.where(low_half == (at == 0), tile, 0.0)
            first = head % group * tok
            qs[head // group, first : first + tok, :] = tile.astype(BF16)
    acc[...] = jnp.zeros_like(acc)

    kvx.take_gathered()
    if gathers:
        wx.take_gathered()

    qpos = me * tok + lax.broadcasted_iota(jnp.int32, (rows, 1), 0) % tok
    unit = lax.broadcasted_iota(jnp.int32, (1, span), 1)

    def attend_to(t, lp):
        base = t * (8 * lp + 1) + (1 - t) * 2 * lp
        stride = 2 * t + 8 * (1 - t)

        @pl.when(base <= me)
        def _():
            kpos = (base + stride * (unit // tok)) * tok + unit % tok

            @each(KVH)
            def _(head):
                kcols = pl.ds(pl.multiple_of(head // 2 * 128, 128), 128)
                vcols = pl.ds(pl.multiple_of(kdim + head // 2 * 128, 128), 128)
                blocks = pl.ds((t * 4 + lp) * 4, 4)
                keys = kv[blocks, :, kcols].reshape(span, 128)
                values = kv[blocks, :, vcols].reshape(span, 128)
                own = (lax.broadcasted_iota(jnp.int32, (span, 128), 1) // HEAD) == head % 2
                value = jnp.where(own, values.astype(F32), 1.0).astype(BF16)
                score = lax.dot_general(
                    qs[head], keys, (((1,), (1,)), ((), ())), preferred_element_type=F32
                )
                expw = jnp.where(kpos <= qpos, jnp.exp2(score), 0.0)
                acc[head] += jnp.dot(
                    expw.astype(BF16),
                    value,
                    preferred_element_type=F32,
                )

    @each(4)
    def _(q):
        by = q + q // 2 - 2 * (q // 3)

        if gathers:

            @pl.when(q == 3)
            def _():
                wx.take_line(1)
                wx.take_line(3)

        @pl.when(q > 0)
        def _():
            kvx.take_line(by)

        attend_to(c, (ln + by) % 4)
        kvx.take_pair((g + by) % 4)
        attend_to(1 - c, (g + by) % 4)

    def mixed(head, offset):
        at = pl.ds(offset * tok, tok)
        both = acc[head, at, :]
        return both / pltpu.roll(both, HEAD, 1)

    for lp in range(4):
        for gp in (0, 2):
            cols = slice((4 * lp + gp) * HEAD, (4 * lp + gp) * HEAD + 128)
            far = slice(1024 + cols.start, 1024 + cols.stop)
            tile = jnp.where(low_half, mixed(gp, 2 * lp), mixed(gp + 1, 2 * lp))
            att[:, cols] = tile.astype(BF16)
            one, two = mixed(lp, 2 * gp + 1), mixed(lp, 2 * gp + 3)
            if lp % 2 == 0:
                two = pltpu.roll(two, HEAD, 1)
            else:
                one = pltpu.roll(one, HEAD, 1)
            att[:, far] = jnp.where(low_half, one, two).astype(BF16)

    if gathers:
        wx.take_line(2)

        @each(4)
        def _(lp):
            wx.take_pair(lp)

        keep.start()
    else:
        fetch.wait()

    for n in range(h_ref.shape[1] // 256):
        cols = slice(n * 256, n * 256 + 256)
        made = jnp.dot(
            att[...], wf[:, :, cols].reshape(QH * HEAD, 256), preferred_element_type=F32
        )
        after_ref[:, cols] = h_ref[:, cols].astype(F32) + made

    kvx.finish()
    if gathers:
        wx.finish()
        keep.wait()


def attend(hidden, attn_gain, q_gain, k_gain, kv_w, w, tick):
    tok, d = hidden.shape
    vmem = pl.BlockSpec(memory_space=pltpu.VMEM)
    hbm = pl.BlockSpec(memory_space=pl.ANY)
    dma = pltpu.SemaphoreType.DMA
    gathers = tick == 0
    after = jax.ShapeDtypeStruct((tok, d), F32)
    whole = jax.ShapeDtypeStruct((32, HEAD, d), BF16)
    sems = [dma((4,)), dma((8,)), dma((4,)), dma((16,)), dma((32,))]
    return pl.pallas_call(
        functools.partial(attn_kernel, gathers),
        out_shape=[after, whole] if gathers else [after],
        in_specs=[vmem] * 5 + [vmem if gathers else hbm],
        out_specs=[vmem, hbm] if gathers else [vmem],
        scratch_shapes=[
            pltpu.VMEM((32, tok, 2 * KVH * HEAD), BF16),
            pltpu.VMEM((KVH, QH // KVH * tok, 128), BF16),
            pltpu.VMEM((KVH, QH // KVH * tok, 128), F32),
            pltpu.VMEM((tok, d), BF16),
            pltpu.VMEM((32, HEAD, d), BF16),
            dma,
            *sems,
            *(sems if gathers else []),
        ],
        compiler_params=pltpu.CompilerParams(
            collective_id=2 + tick, has_side_effects=True, vmem_limit_bytes=56 << 20
        ),
        cost_estimate=pl.CostEstimate(
            flops=40 * 10**9, bytes_accessed=20 * 10**6, transcendentals=10**6
        ),
    )(hidden, attn_gain, q_gain, k_gain, kv_w, w)


def moe_kernel(
    cap,
    tick,
    passes,
    *refs,
):
    if passes:
        after_ref, gain_ref, ids_ref, gates_ref, gu_hbm, dn_hbm, fresh_ref = refs[:7]
        out_ref, next_ref = refs[7:9]
        ob, nb, s5, r5 = refs[-4:]
        refs = refs[9:-4]
    else:
        after_ref, gain_ref, ids_ref, gates_ref, gu_hbm, dn_hbm, out_ref = refs[:7]
        refs = refs[7:]
    (
    xg,
    sb,
    xb,
    bb,
    pb,
    pr,
    pf,
    tot,
    infog,
    sel,
    cw,
    ct,
    gu,
    dn,
    acc,
    hid,
    si,
    ri,
    s1,
    r1,
    s2,
    r2,
    s3,
    r3,
    s4,
    r4,
    wsem,
    ) = refs
    me = lax.axis_index("expert")
    sec = lax.axis_index("section")
    y, z, c = me // 8, (me // 2) % 4, me % 2
    g = c * z + (1 - c) * y
    ln = c * y + (1 - c) * z
    chunks, width = xg.shape[0], xg.shape[3]
    rows = 2 * 4 * cap
    half = 4 * cap
    my_slot = 4 * c + ln
    my_line = 2 * ln + c

    def relay(gp):
        return 2 * (c * (4 * ln + gp) + (1 - c) * (4 * gp + ln)) + c

    def line_dev(i):
        return 2 * (c * (4 * (i // 2) + g) + (1 - c) * (4 * g + i // 2)) + i % 2

    def slot_dev(s):
        t, l0 = s // 4, s % 4
        return (1 - t) * (8 * y + 2 * l0) + t * (8 * l0 + 2 * z + 1)

    def slot_line(s):
        t = s // 4
        return 2 * ((1 - t) * z + t * y) + c

    def remote(src, dst, send, recv, dev):
        return pltpu.make_async_remote_copy(
            src_ref=src,
            dst_ref=dst,
            send_sem=send,
            recv_sem=recv,
            device_id=(sec, dev),
            device_id_type=MESH,
        )

    def info_copy(k):
        gp = (g + k) % 4
        return remote(infog.at[g], infog.at[g], si.at[k], ri.at[g], relay(gp))

    def info_arrival(k):
        gp = (g + k) % 4
        return remote(infog.at[gp], infog.at[gp], si.at[k], ri.at[gp], relay(gp))

    def gather_copy(j, k):
        gp = (g + k) % 4
        return remote(xg.at[j, g], xg.at[j, g], s1.at[j, k], r1.at[j, g], relay(gp))

    def gather_arrival(j, k):
        gp = (g + k) % 4
        return remote(xg.at[j, gp], xg.at[j, gp], s1.at[j, k], r1.at[j, gp], relay(gp))

    def out_copy(j, i):
        return remote(sb.at[j, i], xb.at[j, my_slot], s2.at[j, i], r2.at[j, my_slot], line_dev(i))

    def out_arrival(j, s):
        return remote(xb.at[j, s], xb.at[j, s], s2.at[j, s], r2.at[j, s], slot_dev(s))

    def back_copy(j, s):
        i = slot_line(s)
        return remote(xb.at[j, s], bb.at[j, i], s3.at[j, s], r3.at[j, i], slot_dev(s))

    def back_arrival(j, i):
        return remote(bb.at[j, i], bb.at[j, i], s3.at[j, i], r3.at[j, i], line_dev(i))

    def sum_copy(j, k):
        gp = (g + k) % 4
        return remote(pb.at[j, gp], pr.at[j, g], s4.at[j, k], r4.at[j, g], relay(gp))

    def sum_arrival(j, k):
        gp = (g + k) % 4
        return remote(pr.at[j, gp], pr.at[j, gp], s4.at[j, k], r4.at[j, gp], relay(gp))

    def next_copy(j):
        return pltpu.make_async_remote_copy(
            src_ref=ob.at[j],
            dst_ref=nb.at[j],
            send_sem=s5.at[j],
            recv_sem=r5.at[j],
            device_id=((sec + 1) % 4, me),
            device_id_type=MESH,
        )

    gu_copy = pltpu.make_async_copy(gu_hbm, gu, wsem.at[0])
    dn_copy = pltpu.make_async_copy(dn_hbm, dn, wsem.at[1])

    barrier = pltpu.get_barrier_semaphore()

    def greet(dev):
        pl.semaphore_signal(barrier, inc=1, device_id=(sec, dev), device_id_type=MESH)

    @each(8, 1)
    def _(k):
        greet(8 * y + (2 * z + c + k) % 8)

    @each(4, 1)
    def _(k):
        greet(8 * ((y + k) % 4) + 2 * z)
        greet(8 * ((y + k) % 4) + 2 * z + 1)

    if passes:
        for by in (1, 3):
            pl.semaphore_signal(
                barrier, inc=1, device_id=((sec + by) % 4, me), device_id_type=MESH
            )

    gates = gates_ref[tick].astype(F32) * (1.0 / 1024.0)
    infog[g] = route_info(ids_ref[tick], gates, 64)
    after = after_ref[...]
    scale = lax.rsqrt(jnp.mean(after * after, axis=-1, keepdims=True) + EPS)
    for j in range(chunks):
        cols = slice(j * width, (j + 1) * width)
        xg[j, g] = (after_ref[:, cols] * scale * gain_ref[:, cols]).astype(BF16)
    pl.semaphore_wait(barrier, 15 if passes else 13)

    @each(4, 1)
    def _(k):
        info_copy(k).start()

    @each(chunks)
    def _(j):
        @each(4, 1)
        def _(k):
            gather_copy(j, k).start()

    gu_copy.start()
    dn_copy.start()
    row = lax.broadcasted_iota(jnp.int32, (half, 512), 0)
    lane = lax.broadcasted_iota(jnp.int32, (half, 512), 1)
    block_of_row = (
        (row >= cap).astype(jnp.int32)
        + (row >= 2 * cap).astype(jnp.int32)
        + (row >= 3 * cap).astype(jnp.int32)
    )
    pattern = jnp.where(block_of_row == lane // 128, row - cap * block_of_row, -5).astype(F32)

    @each(4, 1)
    def _(k):
        info_arrival(k).wait_recv()

    def hits(i, e):
        at = 2 * line_dev(i) + e
        rank = jnp.concatenate([infog[b, pl.ds(at, 1), :] for b in range(4)], axis=1)
        return rank == pattern

    @each(8)
    def _(i):
        picks = [jnp.where(hits(i, e), 1.0, 0.0) for e in range(2)]
        at = pl.multiple_of(i * rows, 16)
        sel[pl.ds(at, rows), :] = jnp.concatenate(picks, axis=0).astype(BF16)

    @each(chunks)
    def _(j):
        @each(4, 1)
        def _(k):
            gather_arrival(j, k).wait_recv()

        @each(width // 256)
        def _(n):
            cols = pl.ds(pl.multiple_of(n * 256, 256), 256)
            held = xg[j, :, :, cols].reshape(512, 256)
            got = jnp.dot(sel[...], held, preferred_element_type=F32)
            sb[j, :, :, cols] = got.astype(BF16).reshape(8, rows, 256)

        @each(8, 1)
        def _(k):
            out_copy(j, (my_line + k) % 8).start()

        xb[j, my_slot] = sb[j, my_line]

    @each(8)
    def _(i):
        gates = []
        for e in range(2):
            at = 64 + 2 * line_dev(i) + e
            gate = jnp.concatenate([infog[b, pl.ds(at, 1), :] for b in range(4)], axis=1)
            gates.append(jnp.where(hits(i, e), gate, 0.0))
        at = pl.multiple_of(i * rows, 16)
        cw[pl.ds(at, rows), :] = jnp.concatenate(gates, axis=0).astype(BF16)

    for m in range(8 * rows // 128):
        ct[:, m * 128 : (m + 1) * 128] = (
            cw[m * 128 : (m + 1) * 128, :].astype(F32).T.astype(BF16)
        )

    acc[...] = jnp.zeros_like(acc)
    gu_copy.wait()

    @each(chunks)
    def _(j):
        @each(8, 1)
        def _(k):
            out_arrival(j, (my_slot + k) % 8).wait_recv()

        for e in range(2):
            first = e * (rows - 80)

            @each(acc.shape[2] // 256)
            def _(n):
                cols = pl.ds(pl.multiple_of(n * 256, 256), 256)
                lhs = xb[j, :, first : first + 80, :].reshape(640, width)
                rhs = gu[e, pl.ds(pl.multiple_of(j * width, width), width), cols]
                acc[e, :, cols] += jnp.dot(lhs, rhs, preferred_element_type=F32)

    ff = hid.shape[2]
    for e in range(2):

        @each(640 // 128)
        def _(m):
            at = pl.ds(pl.multiple_of(m * 128, 128), 128)
            hid[e, at, :] = (silu(acc[e, at, :ff]) * acc[e, at, ff:]).astype(BF16)

    dn_copy.wait()

    @each(chunks)
    def _(j):
        @each(width // 256)
        def _(n):
            cols = pl.ds(pl.multiple_of(n * 256, 256), 256)
            at = pl.ds(pl.multiple_of(j * width + n * 256, 256), 256)
            made = [
                jnp.dot(hid[e], dn[e, :, at], preferred_element_type=F32).reshape(8, 80, 256)
                for e in range(2)
            ]
            line = lax.broadcasted_iota(jnp.int32, (8, 16, 256), 1)
            shared = jnp.where(line < 8, made[0][:, 64:80], made[1][:, 0:16])
            xb[j, :, 0:64, cols] = made[0][:, 0:64].astype(BF16)
            xb[j, :, 64:80, cols] = shared.astype(BF16)
            xb[j, :, 80:144, cols] = made[1][:, 16:80].astype(BF16)

        @each(8, 1)
        def _(k):
            back_copy(j, (my_slot + k) % 8).start()

        bb[j, my_line] = xb[j, my_slot]

    @each(chunks)
    def _(j):
        @each(8, 1)
        def _(k):
            back_arrival(j, (my_line + k) % 8).wait_recv()

        @each(width // 256)
        def _(n):
            cols = pl.ds(pl.multiple_of(n * 256, 256), 256)
            at = pl.ds(pl.multiple_of(j * width + n * 256, 256), 256)
            part = jnp.dot(
                ct[...], bb[j, :, :, cols].reshape(8 * rows, 256), preferred_element_type=F32
            ).reshape(4, 128, 256)
            pf[...] = part
            pb[j, :, :, cols] = part.astype(BF16)
            tot[:, at] = after_ref[:, at] + pf[g]

        @each(4, 1)
        def _(k):
            sum_copy(j, k).start()

    @each(chunks)
    def _(j):
        at = pl.ds(pl.multiple_of(j * width, width), width)

        @each(4, 1)
        def _(k):
            sum_arrival(j, k).wait_recv()
            tot[:, at] += pr[j, (g + k) % 4].astype(F32)

        made = tot[:, at].astype(BF16)
        out_ref[:, at] = made
        if passes:
            ob[j] = made
            next_copy(j).start()

    if passes:

        @each(chunks)
        def _(j):
            at = pl.ds(pl.multiple_of(j * width, width), width)
            next_copy(j).wait()
            next_ref[:, at] = jnp.where(sec == 0, fresh_ref[:, at], nb[j])

    @each(4, 1)
    def _(k):
        info_copy(k).wait_send()

    @each(chunks)
    def _(j):
        @each(4, 1)
        def _(k):
            gather_copy(j, k).wait_send()
            sum_copy(j, k).wait_send()

        @each(8, 1)
        def _(k):
            out_copy(j, (my_line + k) % 8).wait_send()
            back_copy(j, (my_slot + k) % 8).wait_send()


def moe_layer(after_attn, gain, ids, gates, gate_up, down, cap, tick, fresh):
    tok, d = after_attn.shape
    ff = down.shape[1]
    w = d // CHUNKS
    rows = 8 * cap
    vmem = pl.BlockSpec(memory_space=pltpu.VMEM)
    hbm = pl.BlockSpec(memory_space=pl.ANY)
    dma = pltpu.SemaphoreType.DMA
    passes = fresh is not None
    outs = 2 if passes else 1
    handed = [
        pltpu.VMEM((CHUNKS, tok, w), BF16),
        pltpu.VMEM((CHUNKS, tok, w), BF16),
        dma((CHUNKS,)),
        dma((CHUNKS,)),
    ]
    return pl.pallas_call(
        functools.partial(moe_kernel, cap, tick, passes),
        out_shape=[jax.ShapeDtypeStruct((tok, d), BF16)] * outs,
        in_specs=[vmem] * 4 + [hbm, hbm] + [vmem] * passes,
        out_specs=[vmem] * outs,
        scratch_shapes=[
            pltpu.VMEM((CHUNKS, 4, tok, w), BF16),
            pltpu.VMEM((CHUNKS, 8, rows, w), BF16),
            pltpu.VMEM((CHUNKS, 8, rows, w), BF16),
            pltpu.VMEM((CHUNKS, 8, rows, w), BF16),
            pltpu.VMEM((CHUNKS, 4, tok, w), BF16),
            pltpu.VMEM((CHUNKS, 4, tok, w), BF16),
            pltpu.VMEM((4, tok, 256), F32),
            pltpu.VMEM((tok, d), F32),
            pltpu.VMEM((4, 128, tok), F32),
            pltpu.VMEM((8 * rows, 4 * tok), BF16),
            pltpu.VMEM((8 * rows, 4 * tok), BF16),
            pltpu.VMEM((4 * tok, 8 * rows), BF16),
            pltpu.VMEM(gate_up.shape, BF16),
            pltpu.VMEM(down.shape, BF16),
            pltpu.VMEM((2, 640, 2 * ff), F32),
            pltpu.VMEM((2, 640, ff), BF16),
            dma((4,)),
            dma((4,)),
            dma((CHUNKS, 4)),
            dma((CHUNKS, 4)),
            dma((CHUNKS, 8)),
            dma((CHUNKS, 8)),
            dma((CHUNKS, 8)),
            dma((CHUNKS, 8)),
            dma((CHUNKS, 4)),
            dma((CHUNKS, 4)),
            dma((2,)),
        ]
        + handed * passes,
        compiler_params=pltpu.CompilerParams(
            collective_id=4 + tick, has_side_effects=True, vmem_limit_bytes=64 << 20
        ),
        cost_estimate=pl.CostEstimate(
            flops=12 * 10**9, bytes_accessed=20 * 10**6, transcendentals=10**6
        ),
    )(after_attn, gain, ids, gates, gate_up, down, *([fresh] if passes else []))


def settle_kernel(first, second, first_out, second_out):
    first_out[...] = first[...]
    second_out[...] = second[...]


def settle(first, second):
    vmem = pl.BlockSpec(memory_space=pltpu.VMEM)
    return pl.pallas_call(
        settle_kernel,
        out_shape=(
            jax.ShapeDtypeStruct(first.shape, first.dtype),
            jax.ShapeDtypeStruct(second.shape, second.dtype),
        ),
        in_specs=[vmem, vmem],
        out_specs=(vmem, vmem),
    )(first, second)


def body(
    section_input,
    fresh_batch,
    attn_gain,
    query_gain,
    key_gain,
    kv_weight,
    out_weight,
    moe_gain,
    expert_gate_up,
    expert_down,
    route_ids,
    route_weights,
):
    devices = lax.axis_size("expert")
    tok = section_input.shape[1]
    experts_all = expert_gate_up.shape[1] * devices
    cap = tok * TOPK * 9 // (8 * experts_all)

    def layer(hidden, tick, w, fresh):
        after_attn, *w = attend(hidden, attn_gain, query_gain, key_gain, kv_weight[0], w, tick)
        outs = moe_layer(
            after_attn,
            moe_gain,
            route_ids[0].transpose(0, 2, 1),
            route_weights[0].transpose(0, 2, 1),
            expert_gate_up[0],
            expert_down[0],
            cap,
            tick,
            fresh,
        )
        return outs, w

    (first_out, second_in), (out_full,) = layer(section_input[0], 0, out_weight[0], fresh_batch)
    (second_out,), _ = layer(second_in, 1, out_full, None)
    return settle(first_out[None], second_out[None])


def solution(mesh):
    in_specs = (
        P("section", "expert", None),
        P("expert", None),
        P("section", None),
        P("section", None),
        P("section", None),
        P("section", None, None),
        P("section", "expert", None),
        P("section", None),
        P("section", "expert", None, None),
        P("section", "expert", None, None),
        P("section", None, "expert", None),
        P("section", None, "expert", None),
    )
    out_specs = (P("section", "expert", None), P("section", "expert", None))
    return jax.shard_map(body, mesh=mesh, in_specs=in_specs, out_specs=out_specs, check_vma=False)
```
